256 devices in a mesh: req: 32 (over y, z), tp: 8 (over x, core).
Axes of the slice: x: 4, y: 4, z: 8, core: 2. Of those that a mesh axis runs over, the one named last changes fastest.
Arguments:
- tokens: bfloat16 [32768, 8192], P('req'), may hold values from -6 to 6
- request_adapter: int32 [32768, 1], P('req'), may hold values from 0 to 255; in each aligned block of 1024 rows (0 to 1023, 1024 to 2047, ...) at most 6 rows name the same one
- storage_position: int32 [256], replicated, may hold values from 0 to 255, each once
- key_value_weight: bfloat16 [8192, 2, 1024], P(None, None, 'tp'), may hold values from -0.0625 to 0.0625
- adapter_down_maps: bfloat16 [256, 8192, 128], P('req', 'tp'), may hold values from -0.0625 to 0.0625
- adapter_up_maps: bfloat16 [256, 2, 64, 1024], P('req', None, None, 'tp'), may hold values from -0.75 to 0.75
Outputs:
- kv_out: bfloat16 [32768, 2, 1024], P('req', None, 'tp')
The draws below stay inside these ranges and needn't reach their ends.
Inputs may be any that keep to these rules, and one draw needn't show every extreme that they name: `request_adapter`: among the rows of one request group no adapter is named by more than 6 rows; in every draw some adapter is named by exactly 6 rows of some group, and every adapter is named somewhere. `storage_position`: each store position once. The panels of store position p are held by request group p // 8.
All inputs are finite; a program needn't handle non-finite values.
Results may differ from the reference program's by a relative error of at most 0.0049.
Values may be sent and summed in bfloat16 or wider, within the bound.
A program may use at most 128 MiB of HBM per device.

```python
import math
import jax
import jax.numpy as jnp
import numpy as np
from jax import lax

MODEL_WIDTH = 8192
ADAPTER_RANK = 64
TOK_DEV = 1024
KEY_VALUE_WIDTH = 1024
ADAPTER_TOTAL = 256
MOST = 6
TOKENS = 32768
N_REQ = 32


def shard_levels(key, dims, shards, least, top_value):
    def one(dim, parts):
        draws = jax.random.uniform(jax.random.fold_in(jax.random.fold_in(key, 6), dim), (parts,), jnp.float32, least / len(shards), top_value / len(shards))
        return jnp.repeat(jnp.exp(draws), dims[dim] // parts).reshape((-1,) + (1,) * (len(dims) - dim - 1))

    gain = one(*shards[0])
    for cut in shards[1:]:
        gain = gain * one(*cut)
    return gain


def routed_block(own_key, own, number, rows, amount, top, limit, slope):
    ranking = jax.random.permutation(own_key, amount)
    heavy_load, ordinary = portions_of(amount, rows * top, limit, slope, True), portions_of(amount, rows * top, limit, slope, False)
    places = jnp.arange(amount)

    def named(sizes, turn):
        used = int((sizes > 0).sum())
        fixed = max(1, used // 4)
        passed = fixed + (places - fixed + turn * (used - fixed)) % max(1, amount - fixed)
        return jnp.zeros((amount,), jnp.int32).at[ranking[jnp.where(places < fixed, places, passed)]].set(jnp.asarray(sizes, jnp.int32))

    sizes = jnp.where(number % 4 == 0, named(heavy_load, number // 4), named(ordinary, number - number // 4 - 1))
    mixed = jax.random.permutation(jax.random.fold_in(own, 3), amount)
    giver, receiver = mixed[0:amount // 2 * 2:2], mixed[1:amount // 2 * 2:2]
    slack = jnp.minimum(sizes[giver] - 1, limit - sizes[receiver]) // 2
    slack = jnp.where((giver == ranking[0]) | (receiver == ranking[0]) | (sizes[receiver] == 0), 0, jnp.maximum(slack, 0))
    passed = jax.random.randint(jax.random.fold_in(own, 4), (amount // 2,), 0, 1 << 20) % (slack + 1)
    sizes = sizes.at[giver].add(-passed).at[receiver].add(passed)
    items = jnp.searchsorted(jnp.cumsum(sizes), jnp.arange(rows * top), side="right").astype(jnp.int32)
    listing = items.reshape(top, rows).T
    listing = listing[jax.random.permutation(jax.random.fold_in(own, 1), rows)]
    turn = jax.random.randint(jax.random.fold_in(own, 2), (rows, 1), 0, top)
    return jnp.take_along_axis(listing, (jnp.arange(top)[None, :] + turn) % top, axis=1)


def portions_of(count, total, limit, slope, full):
    loads = [(1 << 20) // math.isqrt(grade ** slope) + 1 for grade in range(1, count + 1)]
    largest = limit if full else min(limit, max(-(-total // count), total * loads[0] // sum(loads)))
    least = 1 if total - largest >= count - 1 else 0
    holding, spare = [largest] + [least] * (count - 1), total - largest - least * (count - 1)
    while spare > 0:
        candidates = [i for i in range(1, count) if holding[i] < largest] or [i for i in range(1, count) if holding[i] < limit]
        whole, remaining = sum([loads[i] for i in candidates]), spare
        for i in candidates:
            addition = min(limit - holding[i], max(1, remaining * loads[i] // whole), spare)
            holding[i] = holding[i] + addition
            spare = spare - addition
    return np.array(holding)


def gaussian(key, extent, deviation, bound, shards=(), kind=jnp.bfloat16):
    level = shard_levels(key, extent, shards, -0.22, 0.18) if shards else 1.0
    array = jax.random.normal(key, extent, jnp.float32) * deviation * level
    return jnp.minimum(jnp.maximum(array, -bound), bound).astype(kind)


def setup_inputs(seed: int = 0) -> dict:
    keys = jax.random.split(jax.random.key(seed), 7)
    tokens = gaussian(keys[0], (TOKENS, MODEL_WIDTH), 1.0, 6.0, ((0, 32),))
    request_adapter_keys = jax.random.split(jax.random.fold_in(keys[1], 1), TOKENS // TOK_DEV)
    request_adapter_turns = jax.random.permutation(jax.random.fold_in(keys[1], 3), TOKENS // TOK_DEV)
    request_adapter = jax.vmap(lambda own, number: routed_block(jax.random.fold_in(keys[1], 2), own, number, TOK_DEV, ADAPTER_TOTAL, 1, MOST, 2))(request_adapter_keys, request_adapter_turns).reshape((TOKENS, 1))
    storage_position = jax.random.permutation(keys[2], ADAPTER_TOTAL).astype(jnp.int32)
    key_value_weight = gaussian(keys[3], (MODEL_WIDTH, 2, KEY_VALUE_WIDTH), MODEL_WIDTH ** -0.5, 0.0625, ((2, 8),))
    adapter_down_maps = gaussian(keys[4], (ADAPTER_TOTAL, MODEL_WIDTH, 2 * ADAPTER_RANK), MODEL_WIDTH ** -0.5, 0.0625, ((0, 32), (1, 8)))
    adapter_up_maps = gaussian(keys[5], (ADAPTER_TOTAL, 2, ADAPTER_RANK, KEY_VALUE_WIDTH), ADAPTER_RANK ** -0.5, 0.75, ((0, 32), (3, 8)))
    return dict(tokens=tokens, request_adapter=request_adapter, storage_position=storage_position, key_value_weight=key_value_weight, adapter_down_maps=adapter_down_maps, adapter_up_maps=adapter_up_maps)


def reference(tokens, request_adapter, storage_position, key_value_weight, adapter_down_maps, adapter_up_maps):
    base_proj = jnp.dot(tokens, key_value_weight.reshape(MODEL_WIDTH, 2 * KEY_VALUE_WIDTH), preferred_element_type=jnp.float32)
    position = storage_position[request_adapter[:, 0]].astype(jnp.int32)
    capacity = MOST * N_REQ
    padded = jnp.concatenate([tokens, jnp.zeros((1, MODEL_WIDTH), jnp.bfloat16)], axis=0)

    def per_adapter(storage_index):
        chosen_rows = jnp.nonzero(position == storage_index, size=capacity, fill_value=TOKENS)[0].astype(jnp.int32)
        collected_maps = padded[chosen_rows]
        reduced_input = jnp.dot(collected_maps, adapter_down_maps[storage_index], preferred_element_type=jnp.float32).astype(jnp.bfloat16)
        reduced_parts = reduced_input.reshape(capacity, 2, ADAPTER_RANK).astype(jnp.float32)
        update_rows = jnp.einsum("gbt,btn->gbn", reduced_parts, adapter_up_maps[storage_index].astype(jnp.float32)).astype(jnp.bfloat16)
        return chosen_rows, update_rows

    chosen_all, delta_all = lax.map(per_adapter, jnp.arange(ADAPTER_TOTAL, dtype=jnp.int32))
    delta_full = jnp.zeros((TOKENS + 1, 2, KEY_VALUE_WIDTH), jnp.float32)
    delta_full = delta_full.at[chosen_all.reshape(-1)].set(delta_all.reshape(-1, 2, KEY_VALUE_WIDTH).astype(jnp.float32))
    return (base_proj.reshape(TOKENS, 2, KEY_VALUE_WIDTH) + delta_full[:TOKENS]).astype(jnp.bfloat16)
```

```python
import functools

import jax
import jax.numpy as jnp
from jax import lax
from jax.experimental import pallas as pl
from jax.experimental.pallas import tpu as pltpu
from jax.sharding import PartitionSpec as P

MESH = pl.DeviceIdType.MESH
NY, NZ, NT = 4, 8, 8
ORDER = (4, 0, 3, 5, 2, 6, 1, 7)
CHUNKS = len(ORDER) // 2
LOCAL, MOST = 8, 6
PAIR = LOCAL * MOST
SLOTS = 192
BF16, F32 = jnp.bfloat16, jnp.float32


def dot(a, b):
    return jnp.dot(a, b, preferred_element_type=F32)


def kernel(
    tgt_row, tgt_col, code, up, tokens, weight, down, out,
    x, tok, wbuf, w32, amaps, umat, acc,
    packed, meta_out, zin, meta_in, yout, yin, part, rs_in, gath, dout, rin, zret, fin,
    x_sem, a_sem, tok_sem, w_sem,
    z_ss, z_rs, m_ss, m_rs, y_ss, y_rs, r_ss, r_rs, g_ss, g_rs, yr_ss, yr_rs, zr_ss, zr_rs,
):
    group = lax.axis_index("req")
    t = lax.axis_index("tp")
    y, z = group // NZ, group % NZ
    rows, width = x.shape
    full = tokens.shape[1]
    steps = full // width

    def at_z(offset):
        return (y * NZ + lax.rem(z + offset + NZ, NZ), t)

    def at_y(offset):
        return (lax.rem(y + offset + NY, NY) * NZ + z, t)

    def at_t(offset):
        return (group, lax.rem(t + offset, NT))

    barrier = pltpu.get_barrier_semaphore()
    peers = [at_z(d) for d in range(1, NZ)] + [at_y(d) for d in range(1, NY)]
    peers += [at_t(d) for d in range(1, NT)]
    for peer in peers:
        pl.semaphore_signal(barrier, inc=1, device_id=peer, device_id_type=MESH)

    x_copy = pltpu.make_async_copy(
        tokens.at[:, pl.ds(pl.multiple_of(t * width, width), width)], x, x_sem
    )
    x_copy.start()
    a_copy = pltpu.make_async_copy(down, amaps, a_sem)

    def base_copies(step, slot):
        return (
            pltpu.make_async_copy(
                tokens.at[:, pl.ds(pl.multiple_of(step * width, width), width)],
                tok.at[slot], tok_sem.at[slot],
            ),
            pltpu.make_async_copy(
                weight.at[pl.ds(pl.multiple_of(step * 2 * width, 2 * width), 2 * width), :],
                wbuf.at[slot], w_sem.at[slot],
            ),
        )

    def remote(src, dst, ss, rs, peer):
        return pltpu.make_async_remote_copy(
            src_ref=src, dst_ref=dst, send_sem=ss, recv_sem=rs, device_id=peer, device_id_type=MESH
        )

    sent = []
    z_copies, y_copies, r_copies, g_copies, yr_copies, zr_copies = {}, {}, {}, {}, {}, {}

    def pack(k):
        slot_id = lax.broadcasted_iota(jnp.int32, (2 * SLOTS, rows), 0) + 2 * k * SLOTS
        pick = jnp.where(slot_id == tgt_row[...], 1.0, 0.0).astype(BF16)
        codes = lax.dot_general(
            code[...], pick, (((1,), (1,)), ((), ())), preferred_element_type=F32
        )
        for i in range(2):
            q = 2 * k + i
            dst = zin if ORDER[q] == 0 else packed
            mdst = meta_in if ORDER[q] == 0 else meta_out
            mdst[q, :, 0:SLOTS] = codes[:, i * SLOTS : (i + 1) * SLOTS]
        for n in range(width // 256):
            cols = slice(n * 256, (n + 1) * 256)
            block = dot(pick, x[:, cols]).astype(BF16)
            for i in range(2):
                q = 2 * k + i
                dst = zin if ORDER[q] == 0 else packed
                dst[q, :, cols] = block[i * SLOTS : (i + 1) * SLOTS]
        for i in range(2):
            q = 2 * k + i
            if ORDER[q] == 0:
                continue
            peer = at_z(ORDER[q])
            pair = (
                remote(meta_out.at[q], meta_in.at[q], m_ss.at[q], m_rs.at[q], peer),
                remote(packed.at[q], zin.at[q], z_ss.at[q], z_rs.at[q], peer),
            )
            for copy in pair:
                copy.start()
                sent.append(copy)
            z_copies[q] = pair

    def repack(k):
        for i in range(2):
            q = 2 * k + i
            for copy in z_copies.get(q, ()):
                copy.wait_recv()
            want = lax.broadcasted_iota(jnp.int32, (NY * PAIR, SLOTS), 0).astype(F32) + 1.0
            pick = jnp.where(want == meta_in[q, 0:1, 0:SLOTS], 1.0, 0.0).astype(BF16)
            for n in range(width // 256):
                cols = slice(n * 256, (n + 1) * 256)
                block = dot(pick, zin[q, :, cols]).astype(BF16)
                for d in range(NY):
                    dst = yin if d == 0 else yout
                    dst[k, d, i * PAIR : (i + 1) * PAIR, cols] = block[d * PAIR : (d + 1) * PAIR]
        for d in range(1, NY):
            copy = remote(
                yout.at[k, d], yin.at[k, d], y_ss.at[k, d - 1], y_rs.at[k, d - 1], at_y(d)
            )
            copy.start()
            sent.append(copy)
            y_copies[k, d] = copy

    def adapter_of(shape):
        r = lax.broadcasted_iota(jnp.int32, shape, 0)
        return (r % PAIR) // MOST

    chunk_rows = 2 * NY * PAIR

    def project(k):
        for d in range(1, NY):
            y_copies[k, d].wait_recv()
        mine = adapter_of((chunk_rows, 128))

        def body(h, total):
            rhs = jnp.concatenate([amaps[2 * h], amaps[2 * h + 1]], axis=1)
            full_sum = dot(yin[k].reshape(chunk_rows, width), rhs)
            total = total + jnp.where(mine == 2 * h, full_sum[:, :128], 0.0)
            return total + jnp.where(mine == 2 * h + 1, full_sum[:, 128:], 0.0)

        total = lax.fori_loop(0, LOCAL // 2, body, jnp.zeros((chunk_rows, 128), F32))
        part[k] = total.reshape(NT, chunk_rows // NT, 128)
        for d in range(1, NT):
            peer = lax.rem(t + d, NT)
            copy = remote(
                part.at[k, peer], rs_in.at[k, d - 1], r_ss.at[k, d - 1], r_rs.at[k, d - 1], at_t(d)
            )
            copy.start()
            sent.append(copy)
            r_copies[k, d] = copy

    def reduce(k):
        for d in range(1, NT):
            r_copies[k, d].wait_recv()
        total = part[k, t]
        for d in range(1, NT):
            total = total + rs_in[k, d - 1]
        gath[k, t] = total
        for d in range(1, NT):
            copy = remote(
                gath.at[k, t], gath.at[k, t], g_ss.at[k, d - 1], g_rs.at[k, d - 1], at_t(d)
            )
            copy.start()
            sent.append(copy)
            g_copies[k, d] = copy

    def expand(k):
        for d in range(1, NT):
            g_copies[k, d].wait_recv()
        mine = adapter_of((chunk_rows, 128))
        shrunk = gath[k].reshape(chunk_rows, 128)
        spread = jnp.concatenate(
            [jnp.where(mine == e, shrunk, 0.0).astype(BF16) for e in range(LOCAL)], axis=1
        )
        delta = dot(spread, umat[...]).astype(BF16)
        for d in range(NY):
            dst = rin if d == 0 else dout
            dst[k, d] = delta[d * 2 * PAIR : (d + 1) * 2 * PAIR]
        for d in range(1, NY):
            copy = remote(
                dout.at[k, d], rin.at[k, d], yr_ss.at[k, d - 1], yr_rs.at[k, d - 1], at_y(-d)
            )
            copy.start()
            sent.append(copy)
            yr_copies[k, d] = copy

    def unpack(k):
        for d in range(1, NY):
            yr_copies[k, d].wait_recv()
        for i in range(2):
            q = 2 * k + i
            have = jnp.transpose(meta_in[q])[0:SLOTS, 0:1]
            want = lax.broadcasted_iota(jnp.int32, (SLOTS, NY * PAIR), 1).astype(F32) + 1.0
            pick = jnp.where(want == have, 1.0, 0.0).astype(BF16)
            block = jnp.concatenate(
                [rin[k, d, i * PAIR : (i + 1) * PAIR, :] for d in range(NY)], axis=0
            )
            dst = fin if ORDER[q] == 0 else zret
            dst[q] = dot(pick, block).astype(BF16)
            if ORDER[q] == 0:
                continue
            copy = remote(zret.at[q], fin.at[q], zr_ss.at[q], zr_rs.at[q], at_z(-ORDER[q]))
            copy.start()
            sent.append(copy)
            zr_copies[q] = copy

    tile = 256

    def collect(k, last):
        for q in (2 * k, 2 * k + 1):
            if q in zr_copies:
                zr_copies[q].wait_recv()

        def body(r, carry):
            span = pl.ds(pl.multiple_of(r * tile, tile), tile)
            total = acc[span, :]
            for q in (2 * k, 2 * k + 1):
                slot_id = lax.broadcasted_iota(jnp.int32, (tile, SLOTS), 1) + q * SLOTS
                pick = jnp.where(slot_id == tgt_col[span, :], 1.0, 0.0).astype(BF16)
                total = total + dot(pick, fin[q])
            if last:
                out[span, :] = total.astype(BF16)
            else:
                acc[span, :] = total
            return carry

        lax.fori_loop(0, rows // tile, body, 0)

    def base():
        acc[...] = jnp.zeros_like(acc)

        def step(s, carry):
            slot = lax.rem(s, 2)
            for copy in base_copies(s, slot):
                copy.wait()

            @pl.when(s + 1 < steps)
            def _():
                for copy in base_copies(s + 1, 1 - slot):
                    copy.start()

            w32[...] = wbuf[slot].astype(F32)
            rhs = jnp.concatenate(
                [w32[pl.ds(j, width, stride=2), :].astype(BF16) for j in range(2)], axis=1
            )

            def body(r, c):
                span = pl.ds(pl.multiple_of(r * tile, tile), tile)
                acc[span, :] += dot(tok[slot, span, :], rhs)
                return c

            lax.fori_loop(0, rows // tile, body, 0)
            return carry

        lax.fori_loop(0, steps, step, 0)

    rank_row = lax.broadcasted_iota(jnp.int32, up.shape, 0) % 128
    umat[:, 0:128] = jnp.where(rank_row < 64, up[...].astype(F32), 0.0).astype(BF16)
    umat[:, 128:256] = jnp.where(rank_row < 64, 0.0, up[...].astype(F32)).astype(BF16)

    x_copy.wait()
    a_copy.start()
    for copy in base_copies(0, 0):
        copy.start()
    pl.semaphore_wait(barrier, len(peers))
    for k in range(CHUNKS):
        pack(k)
    base()
    a_copy.wait()
    for k in (0, 1):
        repack(k)
        project(k)
        reduce(k)
        expand(k)
        unpack(k)
    repack(2)
    project(2)
    repack(3)
    reduce(2)
    project(3)
    expand(2)
    reduce(3)
    unpack(2)
    expand(3)
    collect(0, False)
    unpack(3)
    collect(1, False)
    collect(2, False)
    collect(3, True)
    for copy in sent:
        copy.wait_send()


def local(
    tokens, request_adapter, storage_position, key_value_weight, adapter_down_maps, adapter_up_maps
):
    rows, full = tokens.shape
    width = adapter_down_maps.shape[1]
    kv = key_value_weight.shape[2]
    adapters = storage_position.shape[0]
    group = lax.axis_index("req")
    y, z = group // NZ, group % NZ
    chosen = request_adapter[:, 0]
    table = jnp.arange(adapters, dtype=jnp.int32)
    position = jnp.sum(
        jnp.where(chosen[:, None] == table[None, :], storage_position[None, :], 0), axis=1
    )
    owner = position // LOCAL
    y_off = (owner // NZ - y + NY) % NY
    z_off = (owner % NZ - z + NZ) % NZ
    seq = jnp.arange(rows, dtype=jnp.int32)
    earlier = seq[None, :] < seq[:, None]
    rank = jnp.sum(((position[:, None] == position[None, :]) & earlier).astype(jnp.int32), axis=1)
    slot = jnp.sum(((z_off[:, None] == z_off[None, :]) & earlier).astype(jnp.int32), axis=1)
    turn = jnp.zeros_like(z_off)
    for q, offset in enumerate(ORDER):
        turn = jnp.where(z_off == offset, q, turn)
    target = turn * SLOTS + slot
    code = (y_off * PAIR + position % LOCAL * MOST + rank + 1).astype(BF16)
    code = jnp.broadcast_to(code[None, :], (8, rows))

    chunk = 2 * NY * PAIR
    vmem = pl.BlockSpec(memory_space=pltpu.VMEM)
    hbm = pl.BlockSpec(memory_space=pl.ANY)
    dma = pltpu.SemaphoreType.DMA
    result = pl.pallas_call(
        kernel,
        out_shape=jax.ShapeDtypeStruct((rows, 2 * kv), BF16),
        in_specs=[vmem, vmem, vmem, vmem, hbm, hbm, hbm],
        out_specs=vmem,
        scratch_shapes=[
            pltpu.VMEM((rows, width), BF16),
            pltpu.VMEM((2, rows, width), BF16),
            pltpu.VMEM((2, 2 * width, kv), BF16),
            pltpu.VMEM((2 * width, kv), F32),
            pltpu.VMEM(adapter_down_maps.shape, BF16),
            pltpu.VMEM((LOCAL * 128, 2 * kv), BF16),
            pltpu.VMEM((rows, 2 * kv), F32),
            pltpu.VMEM((NZ, SLOTS, width), BF16),
            pltpu.VMEM((NZ, 8, 256), F32),
            pltpu.VMEM((NZ, SLOTS, width), BF16),
            pltpu.VMEM((NZ, 8, 256), F32),
            pltpu.VMEM((CHUNKS, NY, 2 * PAIR, width), BF16),
            pltpu.VMEM((CHUNKS, NY, 2 * PAIR, width), BF16),
            pltpu.VMEM((CHUNKS, NT, chunk // NT, 128), F32),
            pltpu.VMEM((CHUNKS, NT - 1, chunk // NT, 128), F32),
            pltpu.VMEM((CHUNKS, NT, chunk // NT, 128), F32),
            pltpu.VMEM((CHUNKS, NY, 2 * PAIR, 2 * kv), BF16),
            pltpu.VMEM((CHUNKS, NY, 2 * PAIR, 2 * kv), BF16),
            pltpu.VMEM((NZ, SLOTS, 2 * kv), BF16),
            pltpu.VMEM((NZ, SLOTS, 2 * kv), BF16),
            dma, dma, dma((2,)), dma((2,)),
            dma((NZ,)), dma((NZ,)), dma((NZ,)), dma((NZ,)),
            dma((CHUNKS, NY - 1)), dma((CHUNKS, NY - 1)),
            dma((CHUNKS, NT - 1)), dma((CHUNKS, NT - 1)),
            dma((CHUNKS, NT - 1)), dma((CHUNKS, NT - 1)),
            dma((CHUNKS, NY - 1)), dma((CHUNKS, NY - 1)),
            dma((NZ,)), dma((NZ,)),
        ],
        compiler_params=pltpu.CompilerParams(
            collective_id=0, has_side_effects=True, vmem_limit_bytes=56 * 2**20
        ),
        cost_estimate=pl.CostEstimate(
            flops=12_000_000_000, bytes_accessed=24_000_000, transcendentals=0
        ),
    )(
        target[None, :], target[:, None], code,
        adapter_up_maps.reshape(LOCAL * 128, kv),
        tokens, key_value_weight.reshape(2 * full, kv), adapter_down_maps,
    )
    return result.reshape(rows, 2, kv)


def solution(mesh):
    in_specs = (
        P("req", None),
        P("req", None),
        P(),
        P(None, None, "tp"),
        P("req", "tp", None),
        P("req", None, None, "tp"),
    )
    out_specs = P("req", None, "tp")
    return jax.shard_map(local, mesh=mesh, in_specs=in_specs, out_specs=out_specs, check_vma=False)
```

```python
import functools

import jax
import jax.numpy as jnp
from jax import lax
from jax.experimental import pallas as pl
from jax.experimental.pallas import tpu as pltpu
from jax.sharding import PartitionSpec as P

MESH = pl.DeviceIdType.MESH
NY, NZ, NT = 4, 8, 8
ORDER = (4, 0, 3, 5, 2, 6, 1, 7)
CHUNKS = len(ORDER) // 2
LOCAL, MOST = 8, 6
PAIR = LOCAL * MOST
POOLED = (4, 3, 5)
SLOTS = 192
SIZE = tuple(SLOTS if d in POOLED else NY * PAIR for d in ORDER)
START = tuple(sum(SIZE[:q]) for q in range(NZ))
BF16, F32 = jnp.bfloat16, jnp.float32


def dot(a, b):
    return jnp.dot(a, b, preferred_element_type=F32)


def kernel(
    tgt_row, tgt_col, code, up, tokens, weight, down, out,
    x, tok, wbuf, w32, amaps, umat, acc,
    packed, meta_out, mid, meta_in, yout, yin, part, rs_in, gath, dout, rmid, zret, fin,
    x_sem, a_sem, tok_sem, w_sem,
    z_ss, z_rs, m_ss, m_rs, y_ss, y_rs, r_ss, r_rs, g_ss, g_rs, yr_ss, yr_rs, zr_ss, zr_rs,
):
    group = lax.axis_index("req")
    t = lax.axis_index("tp")
    y, z = group // NZ, group % NZ
    rows, width = x.shape
    full = tokens.shape[1]
    steps = full // width

    def at_yz(dy, dz):
        return (lax.rem(y + dy + NY, NY) * NZ + lax.rem(z + dz + NZ, NZ), t)

    def at_t(offset):
        return (group, lax.rem(t + offset, NT))

    barrier = pltpu.get_barrier_semaphore()
    pairs = {(0, d) for d in range(1, NZ)} | {(d, 0) for d in range(1, NY)}
    peers = [at_yz(d, e) for d, e in sorted(pairs)] + [at_t(d) for d in range(1, NT)]
    for peer in peers:
        pl.semaphore_signal(barrier, inc=1, device_id=peer, device_id_type=MESH)

    x_copy = pltpu.make_async_copy(
        tokens.at[:, pl.ds(pl.multiple_of(t * width, width), width)], x, x_sem
    )
    x_copy.start()
    a_copy = pltpu.make_async_copy(down, amaps, a_sem)

    def base_copies(step, slot):
        return (
            pltpu.make_async_copy(
                tokens.at[:, pl.ds(pl.multiple_of(step * width, width), width)],
                tok.at[slot], tok_sem.at[slot],
            ),
            pltpu.make_async_copy(
                weight.at[pl.ds(pl.multiple_of(step * 2 * width, 2 * width), 2 * width), :],
                wbuf.at[slot], w_sem.at[slot],
            ),
        )

    def remote(src, dst, ss, rs, peer):
        return pltpu.make_async_remote_copy(
            src_ref=src, dst_ref=dst, send_sem=ss, recv_sem=rs, device_id=peer, device_id_type=MESH
        )

    sent = []
    m_copies, z_copies, y_copies, r_copies, g_copies, yr_copies, zr_copies = ({} for _ in range(7))

    def half(d):
        return pl.ds(d * PAIR, PAIR)

    def send(table, key, copy):
        copy.start()
        sent.append(copy)
        table[key] = copy

    span = pl.ds(0, SLOTS)

    def pack(k):
        count = SIZE[2 * k] + SIZE[2 * k + 1]
        slot_id = lax.broadcasted_iota(jnp.int32, (count, rows), 0) + START[2 * k]
        pick = jnp.where(slot_id == tgt_row[...], 1.0, 0.0).astype(BF16)
        begin = (0, SIZE[2 * k])
        pooled = [i for i in range(2) if ORDER[2 * k + i] in POOLED]
        if pooled:
            codes = lax.dot_general(
                code[...], pick, (((1,), (1,)), ((), ())), preferred_element_type=F32
            )
        for i in pooled:
            meta_out[2 * k + i, :, 0:SLOTS] = codes[:, begin[i] : begin[i] + SLOTS]
        for n in range(width // 256):
            cols = slice(n * 256, (n + 1) * 256)
            block = dot(pick, x[:, cols]).astype(BF16)
            for i in range(2):
                q = 2 * k + i
                packed[q, 0 : SIZE[q], cols] = block[begin[i] : begin[i] + SIZE[q]]
                if i not in pooled:
                    land = yin if ORDER[q] == 0 else mid
                    land[q, 0:PAIR, cols] = block[begin[i] : begin[i] + PAIR]
        for i in range(2):
            q = 2 * k + i
            if i in pooled:
                peer = at_yz(0, ORDER[q])
                send(m_copies, q, remote(meta_out.at[q], meta_in.at[q], m_ss.at[q], m_rs.at[q], peer))
                send(z_copies, q, remote(
                    packed.at[q, span], mid.at[q, span], z_ss.at[q], z_rs.at[q], peer
                ))
                continue
            land = yin if ORDER[q] == 0 else mid
            for d in range(1, NY):
                send(y_copies, (q, d), remote(
                    packed.at[q, half(d)], land.at[q, half(d)],
                    y_ss.at[q, d - 1], y_rs.at[q, d - 1], at_yz(d, 0),
                ))

    def forward(k):
        for q in (2 * k, 2 * k + 1):
            for d in range(1, NY):
                y_copies[q, d].wait_recv()
            send(z_copies, q, remote(
                mid.at[q], yin.at[q], z_ss.at[q], z_rs.at[q], at_yz(0, ORDER[q])
            ))

    def repack(k):
        for q in (2 * k, 2 * k + 1):
            if ORDER[q] not in POOLED:
                continue
            m_copies[q].wait_recv()
            z_copies[q].wait_recv()
            want = lax.broadcasted_iota(jnp.int32, (NY * PAIR, SLOTS), 0).astype(F32) + 1.0
            pick = jnp.where(want == meta_in[q, 0:1, 0:SLOTS], 1.0, 0.0).astype(BF16)
            for n in range(width // 256):
                cols = slice(n * 256, (n + 1) * 256)
                block = dot(pick, mid[q, 0:SLOTS, cols]).astype(BF16)
                yin[q, 0:PAIR, cols] = block[0:PAIR]
                yout[q, :, cols] = block
            for d in range(1, NY):
                send(y_copies, (q, d), remote(
                    yout.at[q, half(d)], yin.at[q, half(d)],
                    y_ss.at[q, d - 1], y_rs.at[q, d - 1], at_yz(d, 0),
                ))

    def adapter_of(shape):
        r = lax.broadcasted_iota(jnp.int32, shape, 0)
        return (r % PAIR) // MOST

    chunk_rows = 2 * NY * PAIR

    def project(k):
        for q in (2 * k, 2 * k + 1):
            if ORDER[q] in POOLED or ORDER[q] == 0:
                for d in range(1, NY):
                    y_copies[q, d].wait_recv()
            else:
                z_copies[q].wait_recv()
        mine = adapter_of((chunk_rows, 128))

        def body(h, total):
            rhs = jnp.concatenate([amaps[2 * h], amaps[2 * h + 1]], axis=1)
            full_sum = dot(yin[2 * k : 2 * k + 2].reshape(chunk_rows, width), rhs)
            total = total + jnp.where(mine == 2 * h, full_sum[:, :128], 0.0)
            return total + jnp.where(mine == 2 * h + 1, full_sum[:, 128:], 0.0)

        total = lax.fori_loop(0, LOCAL // 2, body, jnp.zeros((chunk_rows, 128), F32))
        part[k] = total.reshape(NT, chunk_rows // NT, 128)
        for d in range(1, NT):
            peer = lax.rem(t + d, NT)
            copy = remote(
                part.at[k, peer], rs_in.at[k, d - 1], r_ss.at[k, d - 1], r_rs.at[k, d - 1], at_t(d)
            )
            copy.start()
            sent.append(copy)
            r_copies[k, d] = copy

    def reduce(k):
        for d in range(1, NT):
            r_copies[k, d].wait_recv()
        total = part[k, t]
        for d in range(1, NT):
            total = total + rs_in[k, d - 1]
        gath[k, t] = total.astype(BF16)
        for d in range(1, NT):
            copy = remote(
                gath.at[k, t], gath.at[k, t], g_ss.at[k, d - 1], g_rs.at[k, d - 1], at_t(d)
            )
            copy.start()
            sent.append(copy)
            g_copies[k, d] = copy

    def expand(k):
        for d in range(1, NT):
            g_copies[k, d].wait_recv()
        mine = adapter_of((chunk_rows, 128))
        shrunk = gath[k].reshape(chunk_rows, 128).astype(F32)
        spread = jnp.concatenate(
            [jnp.where(mine == e, shrunk, 0.0).astype(BF16) for e in range(LOCAL)], axis=1
        )
        delta = dot(spread, umat[...]).astype(BF16)
        for i in range(2):
            q = 2 * k + i
            mine = delta[i * NY * PAIR : (i + 1) * NY * PAIR]
            dout[q] = mine
            if ORDER[q] in POOLED or ORDER[q] == 0:
                land = rmid if ORDER[q] in POOLED else fin
                land[q, 0:PAIR] = mine[0:PAIR]
                for d in range(1, NY):
                    send(yr_copies, (q, d), remote(
                        dout.at[q, half(d)], land.at[q, half(d)],
                        yr_ss.at[q, d - 1], yr_rs.at[q, d - 1], at_yz(-d, 0),
                    ))
            else:
                send(zr_copies, q, remote(
                    dout.at[q], rmid.at[q], zr_ss.at[q], zr_rs.at[q], at_yz(0, -ORDER[q])
                ))

    def unpack(k):
        for q in (2 * k, 2 * k + 1):
            if ORDER[q] not in POOLED:
                continue
            for d in range(1, NY):
                yr_copies[q, d].wait_recv()
            have = jnp.transpose(meta_in[q])[0:SLOTS, 0:1]
            want = lax.broadcasted_iota(jnp.int32, (SLOTS, NY * PAIR), 1).astype(F32) + 1.0
            pick = jnp.where(want == have, 1.0, 0.0).astype(BF16)
            zret[q, 0:SLOTS] = dot(pick, rmid[q]).astype(BF16)
            send(zr_copies, q, remote(
                zret.at[q, span], fin.at[q, span], zr_ss.at[q], zr_rs.at[q], at_yz(0, -ORDER[q])
            ))

    def back(k):
        for q in (2 * k, 2 * k + 1):
            zr_copies[q].wait_recv()
            for d in range(1, NY):
                send(yr_copies, (q, d), remote(
                    rmid.at[q, half(d)], fin.at[q, half(d)],
                    yr_ss.at[q, d - 1], yr_rs.at[q, d - 1], at_yz(-d, 0),
                ))
            fin[q, 0:PAIR] = rmid[q, 0:PAIR]

    tile = 256

    def collect(k, last):
        for q in (2 * k, 2 * k + 1):
            if ORDER[q] in POOLED:
                zr_copies[q].wait_recv()
                continue
            for d in range(1, NY):
                yr_copies[q, d].wait_recv()

        def body(r, carry):
            span = pl.ds(pl.multiple_of(r * tile, tile), tile)
            total = acc[span, :]
            for q in (2 * k, 2 * k + 1):
                slot_id = lax.broadcasted_iota(jnp.int32, (tile, SIZE[q]), 1) + START[q]
                pick = jnp.where(slot_id == tgt_col[span, :], 1.0, 0.0).astype(BF16)
                total = total + dot(pick, fin[q, 0 : SIZE[q]])
            if last:
                out[span, :] = total.astype(BF16)
            else:
                acc[span, :] = total
            return carry

        lax.fori_loop(0, rows // tile, body, 0)

    def base(first, stop):
        def step(s, carry):
            slot = lax.rem(s, 2)
            for copy in base_copies(s, slot):
                copy.wait()

            @pl.when(s + 1 < steps)
            def _():
                for copy in base_copies(s + 1, 1 - slot):
                    copy.start()

            w32[...] = wbuf[slot].astype(F32)
            rhs = jnp.concatenate(
                [w32[pl.ds(j, width, stride=2), :].astype(BF16) for j in range(2)], axis=1
            )

            def body(r, c):
                span = pl.ds(pl.multiple_of(r * tile, tile), tile)
                acc[span, :] += dot(tok[slot, span, :], rhs)
                return c

            lax.fori_loop(0, rows // tile, body, 0)
            return carry

        lax.fori_loop(first, stop, step, 0)

    rank_row = lax.broadcasted_iota(jnp.int32, up.shape, 0) % 128
    umat[:, 0:128] = jnp.where(rank_row < 64, up[...].astype(F32), 0.0).astype(BF16)
    umat[:, 128:256] = jnp.where(rank_row < 64, 0.0, up[...].astype(F32)).astype(BF16)

    x_copy.wait()
    a_copy.start()
    for copy in base_copies(0, 0):
        copy.start()
    acc[...] = jnp.zeros_like(acc)
    pl.semaphore_wait(barrier, len(peers))
    pack(0)
    pack(1)
    pack(2)
    pack(3)
    base(0, 4)
    a_copy.wait()
    repack(0)
    forward(2)
    project(0)
    forward(3)
    reduce(0)
    base(4, 6)
    expand(0)
    base(6, 8)
    unpack(0)
    repack(1)
    project(1)
    reduce(1)
    expand(1)
    project(2)
    unpack(1)
    reduce(2)
    project(3)
    expand(2)
    collect(0, False)
    reduce(3)
    back(2)
    expand(3)
    collect(1, False)
    back(3)
    collect(2, False)
    collect(3, True)
    for copy in sent:
        copy.wait_send()


def local(
    tokens, request_adapter, storage_position, key_value_weight, adapter_down_maps, adapter_up_maps
):
    rows, full = tokens.shape
    width = adapter_down_maps.shape[1]
    kv = key_value_weight.shape[2]
    adapters = storage_position.shape[0]
    group = lax.axis_index("req")
    y, z = group // NZ, group % NZ
    chosen = request_adapter[:, 0]
    table = jnp.arange(adapters, dtype=jnp.int32)
    position = jnp.sum(
        jnp.where(chosen[:, None] == table[None, :], storage_position[None, :], 0), axis=1
    )
    owner = position // LOCAL
    y_off = (owner // NZ - y + NY) % NY
    z_off = (owner % NZ - z + NZ) % NZ
    seq = jnp.arange(rows, dtype=jnp.int32)
    earlier = seq[None, :] < seq[:, None]
    rank = jnp.sum(((position[:, None] == position[None, :]) & earlier).astype(jnp.int32), axis=1)
    slot = jnp.sum(((z_off[:, None] == z_off[None, :]) & earlier).astype(jnp.int32), axis=1)
    place = y_off * PAIR + position % LOCAL * MOST + rank
    target = jnp.zeros_like(z_off)
    for q, offset in enumerate(ORDER):
        inside = slot if offset in POOLED else place
        target = jnp.where(z_off == offset, START[q] + inside, target)
    code = jnp.broadcast_to((place + 1).astype(BF16)[None, :], (8, rows))

    chunk = 2 * NY * PAIR
    vmem = pl.BlockSpec(memory_space=pltpu.VMEM)
    hbm = pl.BlockSpec(memory_space=pl.ANY)
    dma = pltpu.SemaphoreType.DMA
    result = pl.pallas_call(
        kernel,
        out_shape=jax.ShapeDtypeStruct((rows, 2 * kv), BF16),
        in_specs=[vmem, vmem, vmem, vmem, hbm, hbm, hbm],
        out_specs=vmem,
        scratch_shapes=[
            pltpu.VMEM((rows, width), BF16),
            pltpu.VMEM((2, rows, width), BF16),
            pltpu.VMEM((2, 2 * width, kv), BF16),
            pltpu.VMEM((2 * width, kv), F32),
            pltpu.VMEM(adapter_down_maps.shape, BF16),
            pltpu.VMEM((LOCAL * 128, 2 * kv), BF16),
            pltpu.VMEM((rows, 2 * kv), F32),
            pltpu.VMEM((NZ, NY * PAIR, width), BF16),
            pltpu.VMEM((NZ, 8, 256), F32),
            pltpu.VMEM((NZ, NY * PAIR, width), BF16),
            pltpu.VMEM((NZ, 8, 256), F32),
            pltpu.VMEM((NZ, NY * PAIR, width), BF16),
            pltpu.VMEM((NZ, NY * PAIR, width), BF16),
            pltpu.VMEM((CHUNKS, NT, chunk // NT, 128), F32),
            pltpu.VMEM((CHUNKS, NT - 1, chunk // NT, 128), F32),
            pltpu.VMEM((CHUNKS, NT, chunk // NT, 128), BF16),
            pltpu.VMEM((NZ, NY * PAIR, 2 * kv), BF16),
            pltpu.VMEM((NZ, NY * PAIR, 2 * kv), BF16),
            pltpu.VMEM((NZ, NY * PAIR, 2 * kv), BF16),
            pltpu.VMEM((NZ, NY * PAIR, 2 * kv), BF16),
            dma, dma, dma((2,)), dma((2,)),
            dma((NZ,)), dma((NZ,)), dma((NZ,)), dma((NZ,)),
            dma((NZ, NY - 1)), dma((NZ, NY - 1)),
            dma((CHUNKS, NT - 1)), dma((CHUNKS, NT - 1)),
            dma((CHUNKS, NT - 1)), dma((CHUNKS, NT - 1)),
            dma((NZ, NY - 1)), dma((NZ, NY - 1)),
            dma((NZ,)), dma((NZ,)),
        ],
        compiler_params=pltpu.CompilerParams(
            collective_id=0, has_side_effects=True, vmem_limit_bytes=56 * 2**20
        ),
        cost_estimate=pl.CostEstimate(
            flops=12_000_000_000, bytes_accessed=24_000_000, transcendentals=0
        ),
    )(
        target[None, :], target[:, None], code,
        adapter_up_maps.reshape(LOCAL * 128, kv),
        tokens, key_value_weight.reshape(2 * full, kv), adapter_down_maps,
    )
    return result.reshape(rows, 2, kv)


def solution(mesh):
    in_specs = (
        P("req", None),
        P("req", None),
        P(),
        P(None, None, "tp"),
        P("req", "tp", None),
        P("req", None, None, "tp"),
    )
    out_specs = P("req", None, "tp")
    return jax.shard_map(local, mesh=mesh, in_specs=in_specs, out_specs=out_specs, check_vma=False)
```

```python
import functools

import jax
import jax.numpy as jnp
from jax import lax
from jax.experimental import pallas as pl
from jax.experimental.pallas import tpu as pltpu
from jax.sharding import PartitionSpec as P

MESH = pl.DeviceIdType.MESH
NY, NZ, NT = 4, 8, 8
ORDER = (4, 0, 3, 5, 2, 6, 1, 7)
CHUNKS = len(ORDER) // 2
LOCAL, MOST = 8, 6
PAIR = LOCAL * MOST
POOLED = (4, 3, 5)
SLOTS = 192
SIZE = tuple(SLOTS if d in POOLED else NY * PAIR for d in ORDER)
START = tuple(sum(SIZE[:q]) for q in range(NZ))
BF16, F32 = jnp.bfloat16, jnp.float32


def dot(a, b):
    return jnp.dot(a, b, preferred_element_type=F32)


def kernel(
    tgt_row, code, up, tokens, weight, down, out,
    x, tok, wbuf, w32, amaps, umat, acc, tgt_col, picks,
    packed, meta_out, mid, meta_in, yout, yin, part, rs_in, gath, dout, rmid, zret, fin,
    x_sem, a_sem, tok_sem, w_sem,
    z_ss, z_rs, m_ss, m_rs, y_ss, y_rs, r_ss, r_rs, g_ss, g_rs, yr_ss, yr_rs, zr_ss, zr_rs,
):
    group = lax.axis_index("req")
    t = lax.axis_index("tp")
    y, z = group // NZ, group % NZ
    rows, width = x.shape
    full = tokens.shape[1]
    steps = full // width

    def at_yz(dy, dz):
        return (lax.rem(y + dy + NY, NY) * NZ + lax.rem(z + dz + NZ, NZ), t)

    def at_t(offset):
        return (group, lax.rem(t + offset, NT))

    barrier = pltpu.get_barrier_semaphore()
    pairs = {(0, d) for d in range(1, NZ)} | {(d, 0) for d in range(1, NY)}
    peers = [at_yz(d, e) for d, e in sorted(pairs)] + [at_t(d) for d in range(1, NT)]
    for peer in peers:
        pl.semaphore_signal(barrier, inc=1, device_id=peer, device_id_type=MESH)

    x_copy = pltpu.make_async_copy(
        tokens.at[:, pl.ds(pl.multiple_of(t * width, width), width)], x, x_sem
    )
    x_copy.start()
    a_copy = pltpu.make_async_copy(down, amaps, a_sem)

    def base_copies(step, slot):
        return (
            pltpu.make_async_copy(
                tokens.at[:, pl.ds(pl.multiple_of(step * width, width), width)],
                tok.at[slot], tok_sem.at[slot],
            ),
            pltpu.make_async_copy(
                weight.at[pl.ds(pl.multiple_of(step * 2 * width, 2 * width), 2 * width), :],
                wbuf.at[slot], w_sem.at[slot],
            ),
        )

    def remote(src, dst, ss, rs, peer):
        return pltpu.make_async_remote_copy(
            src_ref=src, dst_ref=dst, send_sem=ss, recv_sem=rs, device_id=peer, device_id_type=MESH
        )

    sent = []
    m_copies, z_copies, y_copies, r_copies, g_copies, yr_copies, zr_copies = ({} for _ in range(7))

    def half(d):
        return pl.ds(d * PAIR, PAIR)

    def send(table, key, copy):
        copy.start()
        sent.append(copy)
        table[key] = copy

    span = pl.ds(0, SLOTS)

    def pack(k):
        count = SIZE[2 * k] + SIZE[2 * k + 1]
        slot_id = lax.broadcasted_iota(jnp.int32, (count, rows), 0) + START[2 * k]
        pick = jnp.where(slot_id == tgt_row[...], 1.0, 0.0).astype(BF16)
        begin = (0, SIZE[2 * k])
        pooled = [i for i in range(2) if ORDER[2 * k + i] in POOLED]
        if pooled:
            codes = lax.dot_general(
                jnp.broadcast_to(code[...], (8, rows)).astype(BF16), pick,
                (((1,), (1,)), ((), ())), preferred_element_type=F32,
            )
        for i in pooled:
            meta_out[2 * k + i, :, 0:SLOTS] = codes[:, begin[i] : begin[i] + SLOTS]
        if k == 0:
            x_copy.wait()
        for n in range(width // 256):
            cols = slice(n * 256, (n + 1) * 256)
            block = dot(pick, x[:, cols]).astype(BF16)
            for i in range(2):
                q = 2 * k + i
                packed[q, 0 : SIZE[q], cols] = block[begin[i] : begin[i] + SIZE[q]]
                if i not in pooled:
                    land = yin if ORDER[q] == 0 else mid
                    land[q, 0:PAIR, cols] = block[begin[i] : begin[i] + PAIR]
        if k == 0:
            pl.semaphore_wait(barrier, len(peers))
        for i in range(2):
            q = 2 * k + i
            if i in pooled:
                peer = at_yz(0, ORDER[q])
                send(m_copies, q, remote(meta_out.at[q], meta_in.at[q], m_ss.at[q], m_rs.at[q], peer))
                send(z_copies, q, remote(
                    packed.at[q, span], mid.at[q, span], z_ss.at[q], z_rs.at[q], peer
                ))
                continue
            land = yin if ORDER[q] == 0 else mid
            for d in range(1, NY):
                send(y_copies, (q, d), remote(
                    packed.at[q, half(d)], land.at[q, half(d)],
                    y_ss.at[q, d - 1], y_rs.at[q, d - 1], at_yz(d, 0),
                ))

    def forward(k):
        for q in (2 * k, 2 * k + 1):
            for d in range(1, NY):
                y_copies[q, d].wait_recv()
            send(z_copies, q, remote(
                mid.at[q], yin.at[q], z_ss.at[q], z_rs.at[q], at_yz(0, ORDER[q])
            ))

    def repack(k):
        for q in (2 * k, 2 * k + 1):
            if ORDER[q] not in POOLED:
                continue
            m_copies[q].wait_recv()
            z_copies[q].wait_recv()
            want = lax.broadcasted_iota(jnp.int32, (NY * PAIR, SLOTS), 0).astype(F32) + 1.0
            pick = jnp.where(want == meta_in[q, 0:1, 0:SLOTS], 1.0, 0.0).astype(BF16)
            for n in range(width // 256):
                cols = slice(n * 256, (n + 1) * 256)
                block = dot(pick, mid[q, 0:SLOTS, cols]).astype(BF16)
                yin[q, 0:PAIR, cols] = block[0:PAIR]
                yout[q, :, cols] = block
            for d in range(1, NY):
                send(y_copies, (q, d), remote(
                    yout.at[q, half(d)], yin.at[q, half(d)],
                    y_ss.at[q, d - 1], y_rs.at[q, d - 1], at_yz(d, 0),
                ))

    def adapter_of(shape):
        r = lax.broadcasted_iota(jnp.int32, shape, 0)
        return (r % PAIR) // MOST

    chunk_rows = 2 * NY * PAIR

    def project(k):
        for q in (2 * k, 2 * k + 1):
            if ORDER[q] in POOLED or ORDER[q] == 0:
                for d in range(1, NY):
                    y_copies[q, d].wait_recv()
            else:
                z_copies[q].wait_recv()
        mine = adapter_of((chunk_rows, 128))

        def body(h, total):
            rhs = jnp.concatenate([amaps[2 * h], amaps[2 * h + 1]], axis=1)
            full_sum = dot(yin[2 * k : 2 * k + 2].reshape(chunk_rows, width), rhs)
            total = total + jnp.where(mine == 2 * h, full_sum[:, :128], 0.0)
            return total + jnp.where(mine == 2 * h + 1, full_sum[:, 128:], 0.0)

        total = lax.fori_loop(0, LOCAL // 2, body, jnp.zeros((chunk_rows, 128), F32))
        part[k] = total.reshape(NT, chunk_rows // NT, 128)
        for d in range(1, NT):
            peer = lax.rem(t + d, NT)
            copy = remote(
                part.at[k, peer], rs_in.at[k, d - 1], r_ss.at[k, d - 1], r_rs.at[k, d - 1], at_t(d)
            )
            copy.start()
            sent.append(copy)
            r_copies[k, d] = copy

    def reduce(k):
        for d in range(1, NT):
            r_copies[k, d].wait_recv()
        total = part[k, t]
        for d in range(1, NT):
            total = total + rs_in[k, d - 1]
        gath[k, t] = total.astype(BF16)
        for d in range(1, NT):
            copy = remote(
                gath.at[k, t], gath.at[k, t], g_ss.at[k, d - 1], g_rs.at[k, d - 1], at_t(d)
            )
            copy.start()
            sent.append(copy)
            g_copies[k, d] = copy

    def expand(k):
        for d in range(1, NT):
            g_copies[k, d].wait_recv()
        mine = adapter_of((chunk_rows, 128))
        shrunk = gath[k].reshape(chunk_rows, 128).astype(F32)
        spread = jnp.concatenate(
            [jnp.where(mine == e, shrunk, 0.0).astype(BF16) for e in range(LOCAL)], axis=1
        )
        delta = dot(spread, umat[...]).astype(BF16)
        for i in range(2):
            q = 2 * k + i
            mine = delta[i * NY * PAIR : (i + 1) * NY * PAIR]
            dout[q] = mine
            if ORDER[q] in POOLED or ORDER[q] == 0:
                land = rmid if ORDER[q] in POOLED else fin
                land[q, 0:PAIR] = mine[0:PAIR]
                for d in range(1, NY):
                    send(yr_copies, (q, d), remote(
                        dout.at[q, half(d)], land.at[q, half(d)],
                        yr_ss.at[q, d - 1], yr_rs.at[q, d - 1], at_yz(-d, 0),
                    ))
            else:
                send(zr_copies, q, remote(
                    dout.at[q], rmid.at[q], zr_ss.at[q], zr_rs.at[q], at_yz(0, -ORDER[q])
                ))

    def unpack(k):
        for q in (2 * k, 2 * k + 1):
            if ORDER[q] not in POOLED:
                continue
            for d in range(1, NY):
                yr_copies[q, d].wait_recv()
            have = jnp.transpose(meta_in[q])[0:SLOTS, 0:1]
            want = lax.broadcasted_iota(jnp.int32, (SLOTS, NY * PAIR), 1).astype(F32) + 1.0
            pick = jnp.where(want == have, 1.0, 0.0).astype(BF16)
            zret[q, 0:SLOTS] = dot(pick, rmid[q]).astype(BF16)
            send(zr_copies, q, remote(
                zret.at[q, span], fin.at[q, span], zr_ss.at[q], zr_rs.at[q], at_yz(0, -ORDER[q])
            ))

    def back(k):
        for q in (2 * k, 2 * k + 1):
            zr_copies[q].wait_recv()
            for d in range(1, NY):
                send(yr_copies, (q, d), remote(
                    rmid.at[q, half(d)], fin.at[q, half(d)],
                    yr_ss.at[q, d - 1], yr_rs.at[q, d - 1], at_yz(-d, 0),
                ))
            fin[q, 0:PAIR] = rmid[q, 0:PAIR]

    tile = 256

    def collect(k, last):
        for q in (2 * k, 2 * k + 1):
            if ORDER[q] in POOLED:
                zr_copies[q].wait_recv()
                continue
            for d in range(1, NY):
                yr_copies[q, d].wait_recv()

        count = SIZE[2 * k] + SIZE[2 * k + 1]
        rows_in = jnp.concatenate([fin[q, 0 : SIZE[q]] for q in (2 * k, 2 * k + 1)], axis=0)

        def body(r, carry):
            span = pl.ds(pl.multiple_of(r * tile, tile), tile)
            total = acc[span, :] + dot(picks[k, span, 0:count], rows_in)
            if last:
                out[span, :] = total.astype(BF16)
            else:
                acc[span, :] = total
            return carry

        lax.fori_loop(0, rows // tile, body, 0)

    def choose(k):
        count = SIZE[2 * k] + SIZE[2 * k + 1]

        def body(r, carry):
            span = pl.ds(pl.multiple_of(r * tile, tile), tile)
            slot_id = (lax.broadcasted_iota(jnp.int32, (tile, count), 1) + START[2 * k]).astype(F32)
            picks[k, span, 0:count] = jnp.where(slot_id == tgt_col[span, 0:1], 1.0, 0.0).astype(BF16)
            return carry

        lax.fori_loop(0, rows // tile, body, 0)

    def base(first, stop):
        def step(s, carry):
            slot = lax.rem(s, 2)
            for copy in base_copies(s, slot):
                copy.wait()

            @pl.when(s + 1 < steps)
            def _():
                for copy in base_copies(s + 1, 1 - slot):
                    copy.start()

            w32[...] = wbuf[slot].astype(F32)
            rhs = jnp.concatenate(
                [w32[pl.ds(j, width, stride=2), :].astype(BF16) for j in range(2)], axis=1
            )

            def body(r, c):
                span = pl.ds(pl.multiple_of(r * tile, tile), tile)
                acc[span, :] += dot(tok[slot, span, :], rhs)
                return c

            lax.fori_loop(0, rows // tile, body, 0)
            return carry

        lax.fori_loop(first, stop, step, 0)

    pack(0)
    a_copy.start()
    for copy in base_copies(0, 0):
        copy.start()
    pack(1)
    pack(2)
    pack(3)
    rank_row = lax.broadcasted_iota(jnp.int32, up.shape, 0) % 128
    umat[:, 0:128] = jnp.where(rank_row < 64, up[...].astype(F32), 0.0).astype(BF16)
    umat[:, 128:256] = jnp.where(rank_row < 64, 0.0, up[...].astype(F32)).astype(BF16)
    acc[...] = jnp.zeros_like(acc)
    tgt_col[...] = jnp.transpose(jnp.broadcast_to(tgt_row[...].astype(F32), (8, rows)))
    base(0, 5)
    choose(0)
    choose(1)
    a_copy.wait()
    repack(0)
    forward(2)
    project(0)
    forward(3)
    reduce(0)
    base(5, 7)
    expand(0)
    base(7, 8)
    unpack(0)
    repack(1)
    choose(2)
    choose(3)
    project(1)
    reduce(1)
    expand(1)
    project(2)
    unpack(1)
    reduce(2)
    project(3)
    expand(2)
    collect(0, False)
    reduce(3)
    back(2)
    expand(3)
    collect(1, False)
    back(3)
    collect(2, False)
    collect(3, True)
    for copy in sent:
        copy.wait_send()


def local(
    tokens, request_adapter, storage_position, key_value_weight, adapter_down_maps, adapter_up_maps
):
    rows, full = tokens.shape
    width = adapter_down_maps.shape[1]
    kv = key_value_weight.shape[2]
    adapters = storage_position.shape[0]
    group = lax.axis_index("req")
    y, z = group // NZ, group % NZ
    chosen = request_adapter[:, 0]
    table = jnp.arange(adapters, dtype=jnp.int32)
    position = jnp.sum(
        jnp.where(chosen[:, None] == table[None, :], storage_position[None, :], 0), axis=1
    )
    owner = position // LOCAL
    y_off = (owner // NZ - y + NY) % NY
    z_off = (owner % NZ - z + NZ) % NZ
    seq = jnp.arange(rows, dtype=jnp.int32)
    earlier = seq[None, :] < seq[:, None]
    rank = jnp.sum(((position[:, None] == position[None, :]) & earlier).astype(jnp.int32), axis=1)
    slot = jnp.sum(((z_off[:, None] == z_off[None, :]) & earlier).astype(jnp.int32), axis=1)
    place = y_off * PAIR + position % LOCAL * MOST + rank
    target = jnp.zeros_like(z_off)
    for q, offset in enumerate(ORDER):
        inside = slot if offset in POOLED else place
        target = jnp.where(z_off == offset, START[q] + inside, target)
    code = (place + 1).astype(F32)

    chunk = 2 * NY * PAIR
    vmem = pl.BlockSpec(memory_space=pltpu.VMEM)
    hbm = pl.BlockSpec(memory_space=pl.ANY)
    dma = pltpu.SemaphoreType.DMA
    result = pl.pallas_call(
        kernel,
        out_shape=jax.ShapeDtypeStruct((rows, 2 * kv), BF16),
        in_specs=[vmem, vmem, vmem, hbm, hbm, hbm],
        out_specs=vmem,
        scratch_shapes=[
            pltpu.VMEM((rows, width), BF16),
            pltpu.VMEM((2, rows, width), BF16),
            pltpu.VMEM((2, 2 * width, kv), BF16),
            pltpu.VMEM((2 * width, kv), F32),
            pltpu.VMEM(adapter_down_maps.shape, BF16),
            pltpu.VMEM((LOCAL * 128, 2 * kv), BF16),
            pltpu.VMEM((rows, 2 * kv), F32),
            pltpu.VMEM((rows, 8), F32),
            pltpu.VMEM((CHUNKS, rows, 2 * NY * PAIR), BF16),
            pltpu.VMEM((NZ, NY * PAIR, width), BF16),
            pltpu.VMEM((NZ, 8, 256), F32),
            pltpu.VMEM((NZ, NY * PAIR, width), BF16),
            pltpu.VMEM((NZ, 8, 256), F32),
            pltpu.VMEM((NZ, NY * PAIR, width), BF16),
            pltpu.VMEM((NZ, NY * PAIR, width), BF16),
            pltpu.VMEM((CHUNKS, NT, chunk // NT, 128), F32),
            pltpu.VMEM((CHUNKS, NT - 1, chunk // NT, 128), F32),
            pltpu.VMEM((CHUNKS, NT, chunk // NT, 128), BF16),
            pltpu.VMEM((NZ, NY * PAIR, 2 * kv), BF16),
            pltpu.VMEM((NZ, NY * PAIR, 2 * kv), BF16),
            pltpu.VMEM((NZ, NY * PAIR, 2 * kv), BF16),
            pltpu.VMEM((NZ, NY * PAIR, 2 * kv), BF16),
            dma, dma, dma((2,)), dma((2,)),
            dma((NZ,)), dma((NZ,)), dma((NZ,)), dma((NZ,)),
            dma((NZ, NY - 1)), dma((NZ, NY - 1)),
            dma((CHUNKS, NT - 1)), dma((CHUNKS, NT - 1)),
            dma((CHUNKS, NT - 1)), dma((CHUNKS, NT - 1)),
            dma((NZ, NY - 1)), dma((NZ, NY - 1)),
            dma((NZ,)), dma((NZ,)),
        ],
        compiler_params=pltpu.CompilerParams(
            collective_id=0, has_side_effects=True, vmem_limit_bytes=56 * 2**20
        ),
        cost_estimate=pl.CostEstimate(
            flops=12_000_000_000, bytes_accessed=24_000_000, transcendentals=0
        ),
    )(
        target[None, :], code[None, :],
        adapter_up_maps.reshape(LOCAL * 128, kv),
        tokens, key_value_weight.reshape(2 * full, kv), adapter_down_maps,
    )
    return result.reshape(rows, 2, kv)


def solution(mesh):
    in_specs = (
        P("req", None),
        P("req", None),
        P(),
        P(None, None, "tp"),
        P("req", "tp", None),
        P("req", None, None, "tp"),
    )
    out_specs = P("req", None, "tp")
    return jax.shard_map(local, mesh=mesh, in_specs=in_specs, out_specs=out_specs, check_vma=False)
```

```python
import functools

import jax
import jax.numpy as jnp
from jax import lax
from jax.experimental import pallas as pl
from jax.experimental.pallas import tpu as pltpu
from jax.sharding import PartitionSpec as P

MESH = pl.DeviceIdType.MESH
NY, NZ, NT = 4, 8, 8
ORDER = (4, 0, 3, 5, 2, 6, 1, 7)
CHUNKS = len(ORDER) // 2
LOCAL, MOST = 8, 6
PAIR = LOCAL * MOST
POOLED = (4, 3, 5)
SLOTS = 160
SIZE = tuple(SLOTS if d in POOLED else NY * PAIR for d in ORDER)
START = tuple(sum(SIZE[:q]) for q in range(NZ))
BF16, F32 = jnp.bfloat16, jnp.float32


def dot(a, b):
    return jnp.dot(a, b, preferred_element_type=F32)


def kernel(
    tgt_row, code, up, tokens, weight, down, out, over,
    x, tok, wbuf, w32, amaps, umat, acc, tgt_col, picks,
    packed, meta_out, mid, meta_in, yout, yin, part, rs_in, gath, dout, rmid, zret, fin, flags,
    x_sem, a_sem, tok_sem, w_sem,
    z_ss, z_rs, m_ss, m_rs, y_ss, y_rs, r_ss, r_rs, g_ss, g_rs, yr_ss, yr_rs, zr_ss, zr_rs, f_ss, f_rs,
):
    group = lax.axis_index("req")
    t = lax.axis_index("tp")
    y, z = group // NZ, group % NZ
    rows, width = x.shape
    full = tokens.shape[1]
    steps = full // width

    def at_yz(dy, dz):
        return (lax.rem(y + dy + NY, NY) * NZ + lax.rem(z + dz + NZ, NZ), t)

    def at_t(offset):
        return (group, lax.rem(t + offset, NT))

    barrier = pltpu.get_barrier_semaphore()
    pairs = {(0, d) for d in range(1, NZ)} | {(d, 0) for d in range(1, NY)}
    peers = [at_yz(d, e) for d, e in sorted(pairs)] + [at_t(d) for d in range(1, NT)]
    for peer in peers:
        pl.semaphore_signal(barrier, inc=1, device_id=peer, device_id_type=MESH)

    x_copy = pltpu.make_async_copy(
        tokens.at[:, pl.ds(pl.multiple_of(t * width, width), width)], x, x_sem
    )
    x_copy.start()
    a_copy = pltpu.make_async_copy(down, amaps, a_sem)

    def base_copies(step, slot):
        return (
            pltpu.make_async_copy(
                tokens.at[:, pl.ds(pl.multiple_of(step * width, width), width)],
                tok.at[slot], tok_sem.at[slot],
            ),
            pltpu.make_async_copy(
                weight.at[pl.ds(pl.multiple_of(step * 2 * width, 2 * width), 2 * width), :],
                wbuf.at[slot], w_sem.at[slot],
            ),
        )

    def remote(src, dst, ss, rs, peer):
        return pltpu.make_async_remote_copy(
            src_ref=src, dst_ref=dst, send_sem=ss, recv_sem=rs, device_id=peer, device_id_type=MESH
        )

    sent = []
    m_copies, z_copies, y_copies, r_copies, g_copies, yr_copies, zr_copies, f_copies = (
        {} for _ in range(8)
    )

    def half(d):
        return pl.ds(d * PAIR, PAIR)

    def send(table, key, copy):
        copy.start()
        sent.append(copy)
        table[key] = copy

    span = pl.ds(0, SLOTS)

    def pack(k):
        count = SIZE[2 * k] + SIZE[2 * k + 1]
        slot_id = lax.broadcasted_iota(jnp.int32, (count, rows), 0) + START[2 * k]
        pick = jnp.where(slot_id == tgt_row[...], 1.0, 0.0).astype(BF16)
        begin = (0, SIZE[2 * k])
        pooled = [i for i in range(2) if ORDER[2 * k + i] in POOLED]
        if pooled:
            codes = lax.dot_general(
                jnp.broadcast_to(code[...], (8, rows)).astype(BF16), pick,
                (((1,), (1,)), ((), ())), preferred_element_type=F32,
            )
        for i in pooled:
            meta_out[2 * k + i, :, 0:SLOTS] = codes[:, begin[i] : begin[i] + SLOTS]
        if k == 0:
            x_copy.wait()
        for n in range(width // 256):
            cols = slice(n * 256, (n + 1) * 256)
            block = dot(pick, x[:, cols]).astype(BF16)
            for i in range(2):
                q = 2 * k + i
                packed[q, 0 : SIZE[q], cols] = block[begin[i] : begin[i] + SIZE[q]]
                if i not in pooled:
                    land = yin if ORDER[q] == 0 else mid
                    land[q, 0:PAIR, cols] = block[begin[i] : begin[i] + PAIR]
        if k == 0:
            pl.semaphore_wait(barrier, len(peers))
        for i in range(2):
            q = 2 * k + i
            if i in pooled:
                peer = at_yz(0, ORDER[q])
                send(m_copies, q, remote(meta_out.at[q], meta_in.at[q], m_ss.at[q], m_rs.at[q], peer))
                send(z_copies, q, remote(
                    packed.at[q, span], mid.at[q, span], z_ss.at[q], z_rs.at[q], peer
                ))
                continue
            land = yin if ORDER[q] == 0 else mid
            for d in range(1, NY):
                send(y_copies, (q, d), remote(
                    packed.at[q, half(d)], land.at[q, half(d)],
                    y_ss.at[q, d - 1], y_rs.at[q, d - 1], at_yz(d, 0),
                ))

    def forward(k):
        for q in (2 * k, 2 * k + 1):
            for d in range(1, NY):
                y_copies[q, d].wait_recv()
            send(z_copies, q, remote(
                mid.at[q], yin.at[q], z_ss.at[q], z_rs.at[q], at_yz(0, ORDER[q])
            ))

    def repack(k):
        for q in (2 * k, 2 * k + 1):
            if ORDER[q] not in POOLED:
                continue
            m_copies[q].wait_recv()
            z_copies[q].wait_recv()
            want = lax.broadcasted_iota(jnp.int32, (NY * PAIR, SLOTS), 0).astype(F32) + 1.0
            pick = jnp.where(want == meta_in[q, 0:1, 0:SLOTS], 1.0, 0.0).astype(BF16)
            for n in range(width // 256):
                cols = slice(n * 256, (n + 1) * 256)
                block = dot(pick, mid[q, 0:SLOTS, cols]).astype(BF16)
                yin[q, 0:PAIR, cols] = block[0:PAIR]
                yout[q, :, cols] = block
            for d in range(1, NY):
                send(y_copies, (q, d), remote(
                    yout.at[q, half(d)], yin.at[q, half(d)],
                    y_ss.at[q, d - 1], y_rs.at[q, d - 1], at_yz(d, 0),
                ))

    def adapter_of(shape):
        r = lax.broadcasted_iota(jnp.int32, shape, 0)
        return (r % PAIR) // MOST

    chunk_rows = 2 * NY * PAIR

    def project(k):
        for q in (2 * k, 2 * k + 1):
            if ORDER[q] in POOLED or ORDER[q] == 0:
                for d in range(1, NY):
                    y_copies[q, d].wait_recv()
            else:
                z_copies[q].wait_recv()
        mine = adapter_of((chunk_rows, 128))

        def body(h, total):
            rhs = jnp.concatenate([amaps[2 * h], amaps[2 * h + 1]], axis=1)
            full_sum = dot(yin[2 * k : 2 * k + 2].reshape(chunk_rows, width), rhs)
            total = total + jnp.where(mine == 2 * h, full_sum[:, :128], 0.0)
            return total + jnp.where(mine == 2 * h + 1, full_sum[:, 128:], 0.0)

        total = lax.fori_loop(0, LOCAL // 2, body, jnp.zeros((chunk_rows, 128), F32))
        part[k] = total.reshape(NT, chunk_rows // NT, 128)
        for d in range(1, NT):
            peer = lax.rem(t + d, NT)
            copy = remote(
                part.at[k, peer], rs_in.at[k, d - 1], r_ss.at[k, d - 1], r_rs.at[k, d - 1], at_t(d)
            )
            copy.start()
            sent.append(copy)
            r_copies[k, d] = copy

    def reduce(k):
        for d in range(1, NT):
            r_copies[k, d].wait_recv()
        total = part[k, t]
        for d in range(1, NT):
            total = total + rs_in[k, d - 1]
        gath[k, t] = total.astype(BF16)
        for d in range(1, NT):
            copy = remote(
                gath.at[k, t], gath.at[k, t], g_ss.at[k, d - 1], g_rs.at[k, d - 1], at_t(d)
            )
            copy.start()
            sent.append(copy)
            g_copies[k, d] = copy

    def expand(k):
        for d in range(1, NT):
            g_copies[k, d].wait_recv()
        mine = adapter_of((chunk_rows, 128))
        shrunk = gath[k].reshape(chunk_rows, 128).astype(F32)
        spread = jnp.concatenate(
            [jnp.where(mine == e, shrunk, 0.0).astype(BF16) for e in range(LOCAL)], axis=1
        )
        delta = dot(spread, umat[...]).astype(BF16)
        for i in range(2):
            q = 2 * k + i
            mine = delta[i * NY * PAIR : (i + 1) * NY * PAIR]
            dout[q] = mine
            if ORDER[q] in POOLED or ORDER[q] == 0:
                land = rmid if ORDER[q] in POOLED else fin
                land[q, 0:PAIR] = mine[0:PAIR]
                for d in range(1, NY):
                    send(yr_copies, (q, d), remote(
                        dout.at[q, half(d)], land.at[q, half(d)],
                        yr_ss.at[q, d - 1], yr_rs.at[q, d - 1], at_yz(-d, 0),
                    ))
            else:
                send(zr_copies, q, remote(
                    dout.at[q], rmid.at[q], zr_ss.at[q], zr_rs.at[q], at_yz(0, -ORDER[q])
                ))

    def unpack(k):
        for q in (2 * k, 2 * k + 1):
            if ORDER[q] not in POOLED:
                continue
            for d in range(1, NY):
                yr_copies[q, d].wait_recv()
            have = jnp.transpose(meta_in[q])[0:SLOTS, 0:1]
            want = lax.broadcasted_iota(jnp.int32, (SLOTS, NY * PAIR), 1).astype(F32) + 1.0
            pick = jnp.where(want == have, 1.0, 0.0).astype(BF16)
            zret[q, 0:SLOTS] = dot(pick, rmid[q]).astype(BF16)
            send(zr_copies, q, remote(
                zret.at[q, span], fin.at[q, span], zr_ss.at[q], zr_rs.at[q], at_yz(0, -ORDER[q])
            ))

    def back(k):
        for q in (2 * k, 2 * k + 1):
            zr_copies[q].wait_recv()
            for d in range(1, NY):
                send(yr_copies, (q, d), remote(
                    rmid.at[q, half(d)], fin.at[q, half(d)],
                    yr_ss.at[q, d - 1], yr_rs.at[q, d - 1], at_yz(-d, 0),
                ))
            fin[q, 0:PAIR] = rmid[q, 0:PAIR]

    tile = 256

    def collect(k, last):
        for q in (2 * k, 2 * k + 1):
            if ORDER[q] in POOLED:
                zr_copies[q].wait_recv()
                continue
            for d in range(1, NY):
                yr_copies[q, d].wait_recv()

        count = SIZE[2 * k] + SIZE[2 * k + 1]
        rows_in = jnp.concatenate([fin[q, 0 : SIZE[q]] for q in (2 * k, 2 * k + 1)], axis=0)

        def body(r, carry):
            span = pl.ds(pl.multiple_of(r * tile, tile), tile)
            total = acc[span, :] + dot(picks[k, span, 0:count], rows_in)
            if last:
                out[span, :] = total.astype(BF16)
            else:
                acc[span, :] = total
            return carry

        lax.fori_loop(0, rows // tile, body, 0)

    def choose(k):
        count = SIZE[2 * k] + SIZE[2 * k + 1]

        def body(r, carry):
            span = pl.ds(pl.multiple_of(r * tile, tile), tile)
            slot_id = (lax.broadcasted_iota(jnp.int32, (tile, count), 1) + START[2 * k]).astype(F32)
            picks[k, span, 0:count] = jnp.where(slot_id == tgt_col[span, 0:1], 1.0, 0.0).astype(BF16)
            return carry

        lax.fori_loop(0, rows // tile, body, 0)

    def base(first, stop):
        def step(s, carry):
            slot = lax.rem(s, 2)
            for copy in base_copies(s, slot):
                copy.wait()

            @pl.when(s + 1 < steps)
            def _():
                for copy in base_copies(s + 1, 1 - slot):
                    copy.start()

            w32[...] = wbuf[slot].astype(F32)
            rhs = jnp.concatenate(
                [w32[pl.ds(j, width, stride=2), :].astype(BF16) for j in range(2)], axis=1
            )

            def body(r, c):
                span = pl.ds(pl.multiple_of(r * tile, tile), tile)
                acc[span, :] += dot(tok[slot, span, :], rhs)
                return c

            lax.fori_loop(0, rows // tile, body, 0)
            return carry

        lax.fori_loop(first, stop, step, 0)

    pack(0)
    dropped = jnp.where(tgt_row[...] < 0, 1.0, 0.0)
    flags[0] = jnp.broadcast_to(jnp.max(dropped, axis=1, keepdims=True), flags.shape[1:])
    for d in range(1, NZ):
        send(f_copies, d, remote(
            flags.at[0], flags.at[d], f_ss.at[d - 1], f_rs.at[d - 1], at_yz(0, d)
        ))
    a_copy.start()
    for copy in base_copies(0, 0):
        copy.start()
    pack(1)
    pack(2)
    pack(3)
    rank_row = lax.broadcasted_iota(jnp.int32, up.shape, 0) % 128
    umat[:, 0:128] = jnp.where(rank_row < 64, up[...].astype(F32), 0.0).astype(BF16)
    umat[:, 128:256] = jnp.where(rank_row < 64, 0.0, up[...].astype(F32)).astype(BF16)
    acc[...] = jnp.zeros_like(acc)
    tgt_col[...] = jnp.transpose(jnp.broadcast_to(tgt_row[...].astype(F32), (8, rows)))
    base(0, 5)
    for d in range(1, NZ):
        f_copies[d].wait_recv()
    flags[NZ] = jnp.max(flags[0:NZ], axis=0)
    for d in range(1, NY):
        send(f_copies, NZ + d, remote(
            flags.at[NZ], flags.at[NZ + d], f_ss.at[NZ + d - 2], f_rs.at[NZ + d - 2], at_yz(d, 0)
        ))
    choose(0)
    choose(1)
    a_copy.wait()
    repack(0)
    forward(2)
    project(0)
    forward(3)
    reduce(0)
    base(5, 7)
    expand(0)
    base(7, 8)
    unpack(0)
    repack(1)
    choose(2)
    choose(3)
    project(1)
    reduce(1)
    expand(1)
    project(2)
    unpack(1)
    reduce(2)
    project(3)
    expand(2)
    collect(0, False)
    reduce(3)
    back(2)
    expand(3)
    collect(1, False)
    back(3)
    collect(2, False)
    collect(3, True)
    for d in range(1, NY):
        f_copies[NZ + d].wait_recv()
    over[...] = jnp.max(flags[NZ : NZ + NY], axis=0)
    for copy in sent:
        copy.wait_send()


def general(tokens, position, key_value_weight, adapter_down_maps, adapter_up_maps):
    rows, full = tokens.shape
    groups = NY * NZ
    width, rank = adapter_down_maps.shape[1:]
    kv = key_value_weight.shape[2]
    seq = jnp.arange(rows, dtype=jnp.int32)
    earlier = (position[:, None] == position[None, :]) & (seq[None, :] < seq[:, None])
    place = jnp.sum(earlier.astype(jnp.int32), axis=1)
    target = position // LOCAL * PAIR + position % LOCAL * MOST + place
    own = lax.dynamic_slice_in_dim(tokens, lax.axis_index("tp") * width, width, 1)
    outgoing = jnp.zeros((groups * PAIR, width), BF16).at[target].set(own)
    arrived = lax.all_to_all(
        outgoing.reshape(groups, PAIR, width), "req", split_axis=0, concat_axis=0, tiled=True
    )
    partial = jnp.einsum(
        "uebf,efn->uebn", arrived.reshape(groups, LOCAL, MOST, width), adapter_down_maps,
        preferred_element_type=F32,
    )
    shrunk = lax.psum(partial, "tp").astype(BF16)
    delta = jnp.einsum(
        "fipst,istk->fipsk", shrunk.reshape(groups, LOCAL, MOST, 2, rank // 2), adapter_up_maps,
        preferred_element_type=F32,
    ).astype(BF16)
    returned = lax.all_to_all(
        delta.reshape(groups, PAIR, 2, kv), "req", split_axis=0, concat_axis=0, tiled=True
    )
    own_delta = returned.reshape(groups * PAIR, 2, kv)[target]
    base = dot(tokens, key_value_weight.reshape(full, 2 * kv)).reshape(rows, 2, kv)
    return (base + own_delta.astype(F32)).astype(BF16)


def local(
    tokens, request_adapter, storage_position, key_value_weight, adapter_down_maps, adapter_up_maps
):
    rows, full = tokens.shape
    width = adapter_down_maps.shape[1]
    kv = key_value_weight.shape[2]
    adapters = storage_position.shape[0]
    group = lax.axis_index("req")
    y, z = group // NZ, group % NZ
    chosen = request_adapter[:, 0]
    table = jnp.arange(adapters, dtype=jnp.int32)
    position = jnp.sum(
        jnp.where(chosen[:, None] == table[None, :], storage_position[None, :], 0), axis=1
    )
    owner = position // LOCAL
    y_off = (owner // NZ - y + NY) % NY
    z_off = (owner % NZ - z + NZ) % NZ
    seq = jnp.arange(rows, dtype=jnp.int32)
    earlier = seq[None, :] < seq[:, None]
    rank = jnp.sum(((position[:, None] == position[None, :]) & earlier).astype(jnp.int32), axis=1)
    slot = jnp.sum(((z_off[:, None] == z_off[None, :]) & earlier).astype(jnp.int32), axis=1)
    place = y_off * PAIR + position % LOCAL * MOST + rank
    target = jnp.zeros_like(z_off)
    for q, offset in enumerate(ORDER):
        inside = START[q] + place
        if offset in POOLED:
            inside = jnp.where(slot < SLOTS, START[q] + slot, -1)
        target = jnp.where(z_off == offset, inside, target)
    code = (place + 1).astype(F32)

    chunk = 2 * NY * PAIR
    vmem = pl.BlockSpec(memory_space=pltpu.VMEM)
    hbm = pl.BlockSpec(memory_space=pl.ANY)
    dma = pltpu.SemaphoreType.DMA
    result, over = pl.pallas_call(
        kernel,
        out_shape=(
            jax.ShapeDtypeStruct((rows, 2 * kv), BF16),
            jax.ShapeDtypeStruct((8, 128), F32),
        ),
        in_specs=[vmem, vmem, vmem, hbm, hbm, hbm],
        out_specs=(vmem, vmem),
        scratch_shapes=[
            pltpu.VMEM((rows, width), BF16),
            pltpu.VMEM((2, rows, width), BF16),
            pltpu.VMEM((2, 2 * width, kv), BF16),
            pltpu.VMEM((2 * width, kv), F32),
            pltpu.VMEM(adapter_down_maps.shape, BF16),
            pltpu.VMEM((LOCAL * 128, 2 * kv), BF16),
            pltpu.VMEM((rows, 2 * kv), F32),
            pltpu.VMEM((rows, 8), F32),
            pltpu.VMEM((CHUNKS, rows, 2 * NY * PAIR), BF16),
            pltpu.VMEM((NZ, NY * PAIR, width), BF16),
            pltpu.VMEM((NZ, 8, 256), F32),
            pltpu.VMEM((NZ, NY * PAIR, width), BF16),
            pltpu.VMEM((NZ, 8, 256), F32),
            pltpu.VMEM((NZ, NY * PAIR, width), BF16),
            pltpu.VMEM((NZ, NY * PAIR, width), BF16),
            pltpu.VMEM((CHUNKS, NT, chunk // NT, 128), F32),
            pltpu.VMEM((CHUNKS, NT - 1, chunk // NT, 128), F32),
            pltpu.VMEM((CHUNKS, NT, chunk // NT, 128), BF16),
            pltpu.VMEM((NZ, NY * PAIR, 2 * kv), BF16),
            pltpu.VMEM((NZ, NY * PAIR, 2 * kv), BF16),
            pltpu.VMEM((NZ, NY * PAIR, 2 * kv), BF16),
            pltpu.VMEM((NZ, NY * PAIR, 2 * kv), BF16),
            pltpu.VMEM((NZ + NY, 8, 128), F32),
            dma, dma, dma((2,)), dma((2,)),
            dma((NZ,)), dma((NZ,)), dma((NZ,)), dma((NZ,)),
            dma((NZ, NY - 1)), dma((NZ, NY - 1)),
            dma((CHUNKS, NT - 1)), dma((CHUNKS, NT - 1)),
            dma((CHUNKS, NT - 1)), dma((CHUNKS, NT - 1)),
            dma((NZ, NY - 1)), dma((NZ, NY - 1)),
            dma((NZ,)), dma((NZ,)),
            dma((NZ + NY - 2,)), dma((NZ + NY - 2,)),
        ],
        compiler_params=pltpu.CompilerParams(
            collective_id=0, has_side_effects=True, vmem_limit_bytes=56 * 2**20
        ),
        cost_estimate=pl.CostEstimate(
            flops=12_000_000_000, bytes_accessed=24_000_000, transcendentals=0
        ),
    )(
        target[None, :], code[None, :],
        adapter_up_maps.reshape(LOCAL * 128, kv),
        tokens, key_value_weight.reshape(2 * full, kv), adapter_down_maps,
    )
    args = (
        tokens, position, key_value_weight, adapter_down_maps, adapter_up_maps,
    )
    return lax.cond(
        over[0, 0] > 0, lambda: general(*args), lambda: result.reshape(rows, 2, kv)
    )


def solution(mesh):
    in_specs = (
        P("req", None),
        P("req", None),
        P(),
        P(None, None, "tp"),
        P("req", "tp", None),
        P("req", None, None, "tp"),
    )
    out_specs = P("req", None, "tp")
    return jax.shard_map(local, mesh=mesh, in_specs=in_specs, out_specs=out_specs, check_vma=False)
```

```python
import functools

import jax
import jax.numpy as jnp
from jax import lax
from jax.experimental import pallas as pl
from jax.experimental.pallas import tpu as pltpu
from jax.sharding import PartitionSpec as P

MESH = pl.DeviceIdType.MESH
NY, NZ, NT = 4, 8, 8
ORDER = (4, 0, 3, 5, 2, 6, 1, 7)
CHUNKS = len(ORDER) // 2
LOCAL, MOST = 8, 6
PAIR = LOCAL * MOST
POOLED = (4, 3, 5)
SLOTS = 160
SIZE = tuple(SLOTS if d in POOLED else NY * PAIR for d in ORDER)
START = tuple(sum(SIZE[:q]) for q in range(NZ))
BF16, F32 = jnp.bfloat16, jnp.float32


def dot(a, b):
    return jnp.dot(a, b, preferred_element_type=F32)


def kernel(
    chosen, store, up, tokens, weight, down, out, over,
    x, tok, wbuf, w32, amaps, umat, acc, tgt_row, code, tgt_col, picks,
    packed, meta_out, mid, meta_in, yout, yin, part, rs_in, gath, dout, rmid, zret, fin, flags,
    x_sem, a_sem, tok_sem, w_sem,
    z_ss, z_rs, m_ss, m_rs, y_ss, y_rs, r_ss, r_rs, g_ss, g_rs, yr_ss, yr_rs, zr_ss, zr_rs, f_ss, f_rs,
):
    group = lax.axis_index("req")
    t = lax.axis_index("tp")
    y, z = group // NZ, group % NZ
    rows, width = x.shape
    full = tokens.shape[1]
    steps = full // width

    def at_yz(dy, dz):
        return (lax.rem(y + dy + NY, NY) * NZ + lax.rem(z + dz + NZ, NZ), t)

    def at_t(offset):
        return (group, lax.rem(t + offset, NT))

    barrier = pltpu.get_barrier_semaphore()
    pairs = {(0, d) for d in range(1, NZ)} | {(d, 0) for d in range(1, NY)}
    peers = [at_yz(d, e) for d, e in sorted(pairs)] + [at_t(d) for d in range(1, NT)]
    for peer in peers:
        pl.semaphore_signal(barrier, inc=1, device_id=peer, device_id_type=MESH)

    x_copy = pltpu.make_async_copy(
        tokens.at[:, pl.ds(pl.multiple_of(t * width, width), width)], x, x_sem
    )
    x_copy.start()
    a_copy = pltpu.make_async_copy(down, amaps, a_sem)

    def column(row):
        return jnp.transpose(jnp.broadcast_to(row, (8, row.shape[1])))[:, 0:1]

    def assign():
        adapters = store.shape[1]
        table = lax.broadcasted_iota(jnp.int32, (adapters, rows), 0)
        found = jnp.where(table == chosen[...], column(store[...].astype(F32)), 0.0)
        position = jnp.sum(found, axis=0, keepdims=True)
        position_col = column(position)
        place = position.astype(jnp.int32)
        owner, adapter = place >> 3, place & (LOCAL - 1)
        y_off = (owner // NZ - y + NY) & (NY - 1)
        z_to = owner & (NZ - 1)
        z_off = (z_to - z + NZ) & (NZ - 1)
        total = jnp.zeros((1, rows), F32)
        for r in range(rows // 256):
            other = position_col[r * 256 : (r + 1) * 256]
            other_z = (other.astype(jnp.int32) >> 3) & (NZ - 1)
            shape = (256, rows)
            earlier = (
                lax.broadcasted_iota(jnp.int32, shape, 0) + r * 256
                < lax.broadcasted_iota(jnp.int32, shape, 1)
            )
            weight_of = jnp.where(other == position, 2049.0, 1.0)
            counted = jnp.where(earlier & (other_z == z_to), weight_of, 0.0)
            total = total + jnp.sum(counted, axis=0, keepdims=True)
        both = total.astype(jnp.int32)
        rank, slot = both >> 11, both & 2047
        inside = y_off * PAIR + adapter * MOST + rank
        target = jnp.zeros_like(slot)
        for q, offset in enumerate(ORDER):
            here = START[q] + inside
            if offset in POOLED:
                here = jnp.where(slot < SLOTS, START[q] + slot, -1)
            target = jnp.where(z_off == offset, here, target)
        tgt_row[...] = target
        code[...] = (inside + 1).astype(F32)

    def base_copies(step, slot):
        return (
            pltpu.make_async_copy(
                tokens.at[:, pl.ds(pl.multiple_of(step * width, width), width)],
                tok.at[slot], tok_sem.at[slot],
            ),
            pltpu.make_async_copy(
                weight.at[pl.ds(pl.multiple_of(step * 2 * width, 2 * width), 2 * width), :],
                wbuf.at[slot], w_sem.at[slot],
            ),
        )

    def remote(src, dst, ss, rs, peer):
        return pltpu.make_async_remote_copy(
            src_ref=src, dst_ref=dst, send_sem=ss, recv_sem=rs, device_id=peer, device_id_type=MESH
        )

    sent = []
    m_copies, z_copies, y_copies, r_copies, g_copies, yr_copies, zr_copies, f_copies = (
        {} for _ in range(8)
    )

    def half(d):
        return pl.ds(d * PAIR, PAIR)

    def send(table, key, copy):
        copy.start()
        sent.append(copy)
        table[key] = copy

    span = pl.ds(0, SLOTS)

    def pack(k):
        count = SIZE[2 * k] + SIZE[2 * k + 1]
        slot_id = lax.broadcasted_iota(jnp.int32, (count, rows), 0) + START[2 * k]
        pick = jnp.where(slot_id == tgt_row[...], 1.0, 0.0).astype(BF16)
        begin = (0, SIZE[2 * k])
        pooled = [i for i in range(2) if ORDER[2 * k + i] in POOLED]
        if pooled:
            codes = lax.dot_general(
                jnp.broadcast_to(code[...], (8, rows)).astype(BF16), pick,
                (((1,), (1,)), ((), ())), preferred_element_type=F32,
            )
        for i in pooled:
            meta_out[2 * k + i, :, 0:SLOTS] = codes[:, begin[i] : begin[i] + SLOTS]
        if k == 0:
            x_copy.wait()
        for n in range(width // 256):
            cols = slice(n * 256, (n + 1) * 256)
            block = dot(pick, x[:, cols]).astype(BF16)
            for i in range(2):
                q = 2 * k + i
                packed[q, 0 : SIZE[q], cols] = block[begin[i] : begin[i] + SIZE[q]]
                if i not in pooled:
                    land = yin if ORDER[q] == 0 else mid
                    land[q, 0:PAIR, cols] = block[begin[i] : begin[i] + PAIR]
        if k == 0:
            pl.semaphore_wait(barrier, len(peers))
        for i in range(2):
            q = 2 * k + i
            if i in pooled:
                peer = at_yz(0, ORDER[q])
                send(m_copies, q, remote(meta_out.at[q], meta_in.at[q], m_ss.at[q], m_rs.at[q], peer))
                send(z_copies, q, remote(
                    packed.at[q, span], mid.at[q, span], z_ss.at[q], z_rs.at[q], peer
                ))
                continue
            land = yin if ORDER[q] == 0 else mid
            for d in range(1, NY):
                send(y_copies, (q, d), remote(
                    packed.at[q, half(d)], land.at[q, half(d)],
                    y_ss.at[q, d - 1], y_rs.at[q, d - 1], at_yz(d, 0),
                ))

    def forward(k):
        for q in (2 * k, 2 * k + 1):
            for d in range(1, NY):
                y_copies[q, d].wait_recv()
            send(z_copies, q, remote(
                mid.at[q], yin.at[q], z_ss.at[q], z_rs.at[q], at_yz(0, ORDER[q])
            ))

    def repack(k):
        for q in (2 * k, 2 * k + 1):
            if ORDER[q] not in POOLED:
                continue
            m_copies[q].wait_recv()
            z_copies[q].wait_recv()
            want = lax.broadcasted_iota(jnp.int32, (NY * PAIR, SLOTS), 0).astype(F32) + 1.0
            pick = jnp.where(want == meta_in[q, 0:1, 0:SLOTS], 1.0, 0.0).astype(BF16)
            for n in range(width // 256):
                cols = slice(n * 256, (n + 1) * 256)
                block = dot(pick, mid[q, 0:SLOTS, cols]).astype(BF16)
                yin[q, 0:PAIR, cols] = block[0:PAIR]
                yout[q, :, cols] = block
            for d in range(1, NY):
                send(y_copies, (q, d), remote(
                    yout.at[q, half(d)], yin.at[q, half(d)],
                    y_ss.at[q, d - 1], y_rs.at[q, d - 1], at_yz(d, 0),
                ))

    def adapter_of(shape):
        r = lax.broadcasted_iota(jnp.int32, shape, 0)
        return (r % PAIR) // MOST

    chunk_rows = 2 * NY * PAIR

    def project(k):
        for q in (2 * k, 2 * k + 1):
            if ORDER[q] in POOLED or ORDER[q] == 0:
                for d in range(1, NY):
                    y_copies[q, d].wait_recv()
            else:
                z_copies[q].wait_recv()
        mine = adapter_of((chunk_rows, 128))

        def body(h, total):
            rhs = jnp.concatenate([amaps[2 * h], amaps[2 * h + 1]], axis=1)
            full_sum = dot(yin[2 * k : 2 * k + 2].reshape(chunk_rows, width), rhs)
            total = total + jnp.where(mine == 2 * h, full_sum[:, :128], 0.0)
            return total + jnp.where(mine == 2 * h + 1, full_sum[:, 128:], 0.0)

        total = lax.fori_loop(0, LOCAL // 2, body, jnp.zeros((chunk_rows, 128), F32))
        part[k] = total.reshape(NT, chunk_rows // NT, 128)
        for d in range(1, NT):
            peer = lax.rem(t + d, NT)
            copy = remote(
                part.at[k, peer], rs_in.at[k, d - 1], r_ss.at[k, d - 1], r_rs.at[k, d - 1], at_t(d)
            )
            copy.start()
            sent.append(copy)
            r_copies[k, d] = copy

    def reduce(k):
        for d in range(1, NT):
            r_copies[k, d].wait_recv()
        total = part[k, t]
        for d in range(1, NT):
            total = total + rs_in[k, d - 1]
        gath[k, t] = total.astype(BF16)
        for d in range(1, NT):
            copy = remote(
                gath.at[k, t], gath.at[k, t], g_ss.at[k, d - 1], g_rs.at[k, d - 1], at_t(d)
            )
            copy.start()
            sent.append(copy)
            g_copies[k, d] = copy

    def expand(k):
        for d in range(1, NT):
            g_copies[k, d].wait_recv()
        mine = adapter_of((chunk_rows, 128))
        shrunk = gath[k].reshape(chunk_rows, 128).astype(F32)
        spread = jnp.concatenate(
            [jnp.where(mine == e, shrunk, 0.0).astype(BF16) for e in range(LOCAL)], axis=1
        )
        delta = dot(spread, umat[...]).astype(BF16)
        for i in range(2):
            q = 2 * k + i
            mine = delta[i * NY * PAIR : (i + 1) * NY * PAIR]
            dout[q] = mine
            if ORDER[q] in POOLED or ORDER[q] == 0:
                land = rmid if ORDER[q] in POOLED else fin
                land[q, 0:PAIR] = mine[0:PAIR]
                for d in range(1, NY):
                    send(yr_copies, (q, d), remote(
                        dout.at[q, half(d)], land.at[q, half(d)],
                        yr_ss.at[q, d - 1], yr_rs.at[q, d - 1], at_yz(-d, 0),
                    ))
            else:
                send(zr_copies, q, remote(
                    dout.at[q], rmid.at[q], zr_ss.at[q], zr_rs.at[q], at_yz(0, -ORDER[q])
                ))

    def unpack(k):
        for q in (2 * k, 2 * k + 1):
            if ORDER[q] not in POOLED:
                continue
            for d in range(1, NY):
                yr_copies[q, d].wait_recv()
            have = jnp.transpose(meta_in[q])[0:SLOTS, 0:1]
            want = lax.broadcasted_iota(jnp.int32, (SLOTS, NY * PAIR), 1).astype(F32) + 1.0
            pick = jnp.where(want == have, 1.0, 0.0).astype(BF16)
            zret[q, 0:SLOTS] = dot(pick, rmid[q]).astype(BF16)
            send(zr_copies, q, remote(
                zret.at[q, span], fin.at[q, span], zr_ss.at[q], zr_rs.at[q], at_yz(0, -ORDER[q])
            ))

    def back(k):
        for q in (2 * k, 2 * k + 1):
            zr_copies[q].wait_recv()
            for d in range(1, NY):
                send(yr_copies, (q, d), remote(
                    rmid.at[q, half(d)], fin.at[q, half(d)],
                    yr_ss.at[q, d - 1], yr_rs.at[q, d - 1], at_yz(-d, 0),
                ))
            fin[q, 0:PAIR] = rmid[q, 0:PAIR]

    tile = 256

    def collect(k, last):
        for q in (2 * k, 2 * k + 1):
            if ORDER[q] in POOLED:
                zr_copies[q].wait_recv()
                continue
            for d in range(1, NY):
                yr_copies[q, d].wait_recv()

        count = SIZE[2 * k] + SIZE[2 * k + 1]
        rows_in = jnp.concatenate([fin[q, 0 : SIZE[q]] for q in (2 * k, 2 * k + 1)], axis=0)

        def body(r, carry):
            span = pl.ds(pl.multiple_of(r * tile, tile), tile)
            total = acc[span, :] + dot(picks[k, span, 0:count], rows_in)
            if last:
                out[span, :] = total.astype(BF16)
            else:
                acc[span, :] = total
            return carry

        lax.fori_loop(0, rows // tile, body, 0)

    def choose(k):
        count = SIZE[2 * k] + SIZE[2 * k + 1]

        def body(r, carry):
            span = pl.ds(pl.multiple_of(r * tile, tile), tile)
            slot_id = (lax.broadcasted_iota(jnp.int32, (tile, count), 1) + START[2 * k]).astype(F32)
            picks[k, span, 0:count] = jnp.where(slot_id == tgt_col[span, 0:1], 1.0, 0.0).astype(BF16)
            return carry

        lax.fori_loop(0, rows // tile, body, 0)

    def base(first, stop):
        def step(s, carry):
            slot = lax.rem(s, 2)
            for copy in base_copies(s, slot):
                copy.wait()

            @pl.when(s + 1 < steps)
            def _():
                for copy in base_copies(s + 1, 1 - slot):
                    copy.start()

            w32[...] = wbuf[slot].astype(F32)
            rhs = jnp.concatenate(
                [w32[pl.ds(j, width, stride=2), :].astype(BF16) for j in range(2)], axis=1
            )

            def body(r, c):
                span = pl.ds(pl.multiple_of(r * tile, tile), tile)
                acc[span, :] += dot(tok[slot, span, :], rhs)
                return c

            lax.fori_loop(0, rows // tile, body, 0)
            return carry

        lax.fori_loop(first, stop, step, 0)

    assign()
    pack(0)
    dropped = jnp.where(tgt_row[...] < 0, 1.0, 0.0)
    flags[0] = jnp.broadcast_to(jnp.max(dropped, axis=1, keepdims=True), flags.shape[1:])
    for d in range(1, NZ):
        send(f_copies, d, remote(
            flags.at[0], flags.at[d], f_ss.at[d - 1], f_rs.at[d - 1], at_yz(0, d)
        ))
    a_copy.start()
    for copy in base_copies(0, 0):
        copy.start()
    pack(1)
    pack(2)
    pack(3)
    rank_row = lax.broadcasted_iota(jnp.int32, up.shape, 0) % 128
    umat[:, 0:128] = jnp.where(rank_row < 64, up[...].astype(F32), 0.0).astype(BF16)
    umat[:, 128:256] = jnp.where(rank_row < 64, 0.0, up[...].astype(F32)).astype(BF16)
    acc[...] = jnp.zeros_like(acc)
    tgt_col[...] = jnp.transpose(jnp.broadcast_to(tgt_row[...].astype(F32), (8, rows)))
    base(0, 5)
    for d in range(1, NZ):
        f_copies[d].wait_recv()
    flags[NZ] = jnp.max(flags[0:NZ], axis=0)
    for d in range(1, NY):
        send(f_copies, NZ + d, remote(
            flags.at[NZ], flags.at[NZ + d], f_ss.at[NZ + d - 2], f_rs.at[NZ + d - 2], at_yz(d, 0)
        ))
    choose(0)
    choose(1)
    a_copy.wait()
    repack(0)
    forward(2)
    project(0)
    forward(3)
    reduce(0)
    base(5, 7)
    expand(0)
    base(7, 8)
    unpack(0)
    repack(1)
    choose(2)
    choose(3)
    project(1)
    reduce(1)
    project(2)
    expand(1)
    reduce(2)
    project(3)
    unpack(1)
    expand(2)
    collect(0, False)
    reduce(3)
    collect(1, False)
    expand(3)
    back(2)
    back(3)
    collect(2, False)
    collect(3, True)
    for d in range(1, NY):
        f_copies[NZ + d].wait_recv()
    over[0, 0] = jnp.max(flags[NZ : NZ + NY])
    for copy in sent:
        copy.wait_send()


def general(
    tokens, request_adapter, storage_position, key_value_weight, adapter_down_maps, adapter_up_maps
):
    rows, full = tokens.shape
    groups = NY * NZ
    width, rank = adapter_down_maps.shape[1:]
    kv = key_value_weight.shape[2]
    table = jnp.arange(storage_position.shape[0], dtype=jnp.int32)
    position = jnp.sum(
        jnp.where(request_adapter == table[None, :], storage_position[None, :], 0), axis=1
    )
    seq = jnp.arange(rows, dtype=jnp.int32)
    earlier = (position[:, None] == position[None, :]) & (seq[None, :] < seq[:, None])
    place = jnp.sum(earlier.astype(jnp.int32), axis=1)
    target = position // LOCAL * PAIR + position % LOCAL * MOST + place
    own = lax.dynamic_slice_in_dim(tokens, lax.axis_index("tp") * width, width, 1)
    outgoing = jnp.zeros((groups * PAIR, width), BF16).at[target].set(own)
    arrived = lax.all_to_all(
        outgoing.reshape(groups, PAIR, width), "req", split_axis=0, concat_axis=0, tiled=True
    )
    partial = jnp.einsum(
        "uebf,efn->uebn", arrived.reshape(groups, LOCAL, MOST, width), adapter_down_maps,
        preferred_element_type=F32,
    )
    shrunk = lax.psum(partial, "tp").astype(BF16)
    delta = jnp.einsum(
        "fipst,istk->fipsk", shrunk.reshape(groups, LOCAL, MOST, 2, rank // 2), adapter_up_maps,
        preferred_element_type=F32,
    ).astype(BF16)
    returned = lax.all_to_all(
        delta.reshape(groups, PAIR, 2, kv), "req", split_axis=0, concat_axis=0, tiled=True
    )
    own_delta = returned.reshape(groups * PAIR, 2, kv)[target]
    base = dot(tokens, key_value_weight.reshape(full, 2 * kv)).reshape(rows, 2, kv)
    return (base + own_delta.astype(F32)).astype(BF16)


def local(
    tokens, request_adapter, storage_position, key_value_weight, adapter_down_maps, adapter_up_maps
):
    rows, full = tokens.shape
    width = adapter_down_maps.shape[1]
    kv = key_value_weight.shape[2]
    adapters = storage_position.shape[0]
    chunk = 2 * NY * PAIR
    vmem = pl.BlockSpec(memory_space=pltpu.VMEM)
    hbm = pl.BlockSpec(memory_space=pl.ANY)
    dma = pltpu.SemaphoreType.DMA
    result, over = pl.pallas_call(
        kernel,
        out_shape=(
            jax.ShapeDtypeStruct((rows, 2 * kv), BF16),
            jax.ShapeDtypeStruct((1, 1), F32),
        ),
        in_specs=[vmem, vmem, vmem, hbm, hbm, hbm],
        out_specs=(vmem, pl.BlockSpec(memory_space=pltpu.SMEM)),
        scratch_shapes=[
            pltpu.VMEM((rows, width), BF16),
            pltpu.VMEM((2, rows, width), BF16),
            pltpu.VMEM((2, 2 * width, kv), BF16),
            pltpu.VMEM((2 * width, kv), F32),
            pltpu.VMEM(adapter_down_maps.shape, BF16),
            pltpu.VMEM((LOCAL * 128, 2 * kv), BF16),
            pltpu.VMEM((rows, 2 * kv), F32),
            pltpu.VMEM((1, rows), jnp.int32),
            pltpu.VMEM((1, rows), F32),
            pltpu.VMEM((rows, 8), F32),
            pltpu.VMEM((CHUNKS, rows, 2 * NY * PAIR), BF16),
            pltpu.VMEM((NZ, NY * PAIR, width), BF16),
            pltpu.VMEM((NZ, 8, 256), F32),
            pltpu.VMEM((NZ, NY * PAIR, width), BF16),
            pltpu.VMEM((NZ, 8, 256), F32),
            pltpu.VMEM((NZ, NY * PAIR, width), BF16),
            pltpu.VMEM((NZ, NY * PAIR, width), BF16),
            pltpu.VMEM((CHUNKS, NT, chunk // NT, 128), F32),
            pltpu.VMEM((CHUNKS, NT - 1, chunk // NT, 128), F32),
            pltpu.VMEM((CHUNKS, NT, chunk // NT, 128), BF16),
            pltpu.VMEM((NZ, NY * PAIR, 2 * kv), BF16),
            pltpu.VMEM((NZ, NY * PAIR, 2 * kv), BF16),
            pltpu.VMEM((NZ, NY * PAIR, 2 * kv), BF16),
            pltpu.VMEM((NZ, NY * PAIR, 2 * kv), BF16),
            pltpu.VMEM((NZ + NY, 8, 128), F32),
            dma, dma, dma((2,)), dma((2,)),
            dma((NZ,)), dma((NZ,)), dma((NZ,)), dma((NZ,)),
            dma((NZ, NY - 1)), dma((NZ, NY - 1)),
            dma((CHUNKS, NT - 1)), dma((CHUNKS, NT - 1)),
            dma((CHUNKS, NT - 1)), dma((CHUNKS, NT - 1)),
            dma((NZ, NY - 1)), dma((NZ, NY - 1)),
            dma((NZ,)), dma((NZ,)),
            dma((NZ + NY - 2,)), dma((NZ + NY - 2,)),
        ],
        compiler_params=pltpu.CompilerParams(
            collective_id=0, has_side_effects=True, vmem_limit_bytes=56 * 2**20
        ),
        cost_estimate=pl.CostEstimate(
            flops=12_000_000_000, bytes_accessed=24_000_000, transcendentals=0
        ),
    )(
        request_adapter.reshape(1, rows), storage_position.reshape(1, adapters),
        adapter_up_maps.reshape(LOCAL * 128, kv),
        tokens, key_value_weight.reshape(2 * full, kv), adapter_down_maps,
    )
    args = (
        tokens, request_adapter, storage_position, key_value_weight, adapter_down_maps,
        adapter_up_maps,
    )
    return lax.cond(
        over[0, 0] > 0, lambda: general(*args), lambda: result.reshape(rows, 2, kv)
    )


def solution(mesh):
    in_specs = (
        P("req", None),
        P("req", None),
        P(),
        P(None, None, "tp"),
        P("req", "tp", None),
        P("req", None, None, "tp"),
    )
    out_specs = P("req", None, "tp")
    return jax.shard_map(local, mesh=mesh, in_specs=in_specs, out_specs=out_specs, check_vma=False)
```

```python
import functools

import jax
import jax.numpy as jnp
from jax import lax
from jax.experimental import pallas as pl
from jax.experimental.pallas import tpu as pltpu
from jax.sharding import PartitionSpec as P

MESH = pl.DeviceIdType.MESH
NY, NZ, NT = 4, 8, 8
ORDER = (4, 0, 3, 5, 2, 6, 1, 7)
CHUNKS = len(ORDER) // 2
LOCAL, MOST = 8, 6
PAIR = LOCAL * MOST
POOLED = (4, 3, 5)
SLOTS = 160
SIZE = tuple(SLOTS if d in POOLED else NY * PAIR for d in ORDER)
START = tuple(sum(SIZE[:q]) for q in range(NZ))
BF16, F32 = jnp.bfloat16, jnp.float32


def dot(a, b):
    return jnp.dot(a, b, preferred_element_type=F32)


def kernel(
    chosen, store, up, tokens, weight, down, out, over,
    x, tok, wbuf, w32, amaps, umat, acc, tgt_row, code, tgt_col, picks,
    packed, meta_out, mid, meta_in, yout, yin, part, rs_in, gath, dout, rmid, zret, fin, flags,
    x_sem, a_sem, tok_sem, w_sem,
    z_ss, z_rs, m_ss, m_rs, y_ss, y_rs, r_ss, r_rs, g_ss, g_rs, yr_ss, yr_rs, zr_ss, zr_rs, f_ss, f_rs,
):
    group = lax.axis_index("req")
    t = lax.axis_index("tp")
    y, z = group // NZ, group % NZ
    rows, width = x.shape
    full = tokens.shape[1]
    steps = full // width

    def at_yz(dy, dz):
        return (lax.rem(y + dy + NY, NY) * NZ + lax.rem(z + dz + NZ, NZ), t)

    def at_t(offset):
        return (group, lax.rem(t + offset, NT))

    barrier = pltpu.get_barrier_semaphore()
    pairs = {(0, d) for d in range(1, NZ)} | {(d, 0) for d in range(1, NY)}
    peers = [at_yz(d, e) for d, e in sorted(pairs)] + [at_t(d) for d in range(1, NT)]
    for peer in peers:
        pl.semaphore_signal(barrier, inc=1, device_id=peer, device_id_type=MESH)

    x_copy = pltpu.make_async_copy(
        tokens.at[:, pl.ds(pl.multiple_of(t * width, width), width)], x, x_sem
    )
    x_copy.start()
    a_copy = pltpu.make_async_copy(down, amaps, a_sem)

    def column(row):
        return jnp.transpose(jnp.broadcast_to(row, (8, row.shape[1])))[:, 0:1]

    def assign():
        adapters = store.shape[1]
        table = lax.broadcasted_iota(jnp.int32, (adapters, rows), 0)
        found = jnp.where(table == chosen[...], column(store[...].astype(F32)), 0.0)
        position = jnp.sum(found, axis=0, keepdims=True)
        position_col = column(position)
        place = position.astype(jnp.int32)
        owner, adapter = place >> 3, place & (LOCAL - 1)
        y_off = (owner // NZ - y + NY) & (NY - 1)
        z_to = owner & (NZ - 1)
        z_off = (z_to - z + NZ) & (NZ - 1)
        side = 256
        spans = [slice(r * side, (r + 1) * side) for r in range(rows // side)]
        other = [position_col[span] for span in spans]
        other_z = [(o.astype(jnp.int32) >> 3) & (NZ - 1) for o in other]
        before = lax.broadcasted_iota(jnp.int32, (side, side), 0) < lax.broadcasted_iota(
            jnp.int32, (side, side), 1
        )
        totals = []
        for j, span in enumerate(spans):
            total = jnp.zeros((1, side), F32)
            for r in range(j + 1):
                counted = jnp.where(other[r] == position[:, span], 2049.0, 1.0)
                counted = jnp.where(other_z[r] == z_to[:, span], counted, 0.0)
                if r == j:
                    counted = jnp.where(before, counted, 0.0)
                total = total + jnp.sum(counted, axis=0, keepdims=True)
            totals.append(total)
        total = jnp.concatenate(totals, axis=1)
        both = total.astype(jnp.int32)
        rank, slot = both >> 11, both & 2047
        inside = y_off * PAIR + adapter * MOST + rank
        target = jnp.zeros_like(slot)
        for q, offset in enumerate(ORDER):
            here = START[q] + inside
            if offset in POOLED:
                here = jnp.where(slot < SLOTS, START[q] + slot, -1)
            target = jnp.where(z_off == offset, here, target)
        tgt_row[...] = target
        code[...] = (inside + 1).astype(F32)

    def base_copies(step, slot):
        return (
            pltpu.make_async_copy(
                tokens.at[:, pl.ds(pl.multiple_of(step * width, width), width)],
                tok.at[slot], tok_sem.at[slot],
            ),
            pltpu.make_async_copy(
                weight.at[pl.ds(pl.multiple_of(step * 2 * width, 2 * width), 2 * width), :],
                wbuf.at[slot], w_sem.at[slot],
            ),
        )

    def remote(src, dst, ss, rs, peer):
        return pltpu.make_async_remote_copy(
            src_ref=src, dst_ref=dst, send_sem=ss, recv_sem=rs, device_id=peer, device_id_type=MESH
        )

    sent = []
    m_copies, z_copies, y_copies, r_copies, g_copies, yr_copies, zr_copies, f_copies = (
        {} for _ in range(8)
    )

    def half(d):
        return pl.ds(d * PAIR, PAIR)

    def send(table, key, copy):
        copy.start()
        sent.append(copy)
        table[key] = copy

    span = pl.ds(0, SLOTS)

    def pack(*turns):
        count = sum(SIZE[q] for q in turns)
        slot_id = lax.broadcasted_iota(jnp.int32, (count, rows), 0) + START[turns[0]]
        pick = jnp.where(slot_id == tgt_row[...], 1.0, 0.0).astype(BF16)
        first = 0 in turns
        if first:
            x_copy.wait()
        for n in range(width // 256):
            cols = slice(n * 256, (n + 1) * 256)
            block = dot(pick, x[:, cols]).astype(BF16)
            for q in turns:
                begin = START[q] - START[turns[0]]
                packed[q, 0 : SIZE[q], cols] = block[begin : begin + SIZE[q]]
                if ORDER[q] not in POOLED:
                    land = yin if ORDER[q] == 0 else mid
                    land[q, 0:PAIR, cols] = block[begin : begin + PAIR]
        if first:
            pl.semaphore_wait(barrier, len(peers))
        for q in turns:
            if ORDER[q] in POOLED:
                send(z_copies, q, remote(
                    packed.at[q, span], mid.at[q, span], z_ss.at[q], z_rs.at[q],
                    at_yz(0, ORDER[q]),
                ))
                continue
            land = yin if ORDER[q] == 0 else mid
            for d in range(1, NY):
                send(y_copies, (q, d), remote(
                    packed.at[q, half(d)], land.at[q, half(d)],
                    y_ss.at[q, d - 1], y_rs.at[q, d - 1], at_yz(d, 0),
                ))
        pooled = [q for q in turns if ORDER[q] in POOLED]
        if pooled:
            codes = lax.dot_general(
                jnp.broadcast_to(code[...], (8, rows)).astype(BF16), pick,
                (((1,), (1,)), ((), ())), preferred_element_type=F32,
            )
        for q in pooled:
            begin = START[q] - START[turns[0]]
            meta_out[q, :, 0:SLOTS] = codes[:, begin : begin + SLOTS]
            send(m_copies, q, remote(
                meta_out.at[q], meta_in.at[q], m_ss.at[q], m_rs.at[q], at_yz(0, ORDER[q])
            ))

    def forward(k):
        for q in (2 * k, 2 * k + 1):
            for d in range(1, NY):
                y_copies[q, d].wait_recv()
            send(z_copies, q, remote(
                mid.at[q], yin.at[q], z_ss.at[q], z_rs.at[q], at_yz(0, ORDER[q])
            ))

    def repack(k):
        for q in (2 * k, 2 * k + 1):
            if ORDER[q] not in POOLED:
                continue
            m_copies[q].wait_recv()
            z_copies[q].wait_recv()
            want = lax.broadcasted_iota(jnp.int32, (NY * PAIR, SLOTS), 0).astype(F32) + 1.0
            pick = jnp.where(want == meta_in[q, 0:1, 0:SLOTS], 1.0, 0.0).astype(BF16)
            for n in range(width // 256):
                cols = slice(n * 256, (n + 1) * 256)
                block = dot(pick, mid[q, 0:SLOTS, cols]).astype(BF16)
                yin[q, 0:PAIR, cols] = block[0:PAIR]
                yout[q, :, cols] = block
            for d in range(1, NY):
                send(y_copies, (q, d), remote(
                    yout.at[q, half(d)], yin.at[q, half(d)],
                    y_ss.at[q, d - 1], y_rs.at[q, d - 1], at_yz(d, 0),
                ))

    def adapter_of(shape):
        r = lax.broadcasted_iota(jnp.int32, shape, 0)
        return (r % PAIR) // MOST

    chunk_rows = 2 * NY * PAIR

    def project(k):
        for q in (2 * k, 2 * k + 1):
            if ORDER[q] in POOLED or ORDER[q] == 0:
                for d in range(1, NY):
                    y_copies[q, d].wait_recv()
            else:
                z_copies[q].wait_recv()
        mine = adapter_of((chunk_rows, 128))

        def body(h, total):
            rhs = jnp.concatenate([amaps[2 * h], amaps[2 * h + 1]], axis=1)
            full_sum = dot(yin[2 * k : 2 * k + 2].reshape(chunk_rows, width), rhs)
            total = total + jnp.where(mine == 2 * h, full_sum[:, :128], 0.0)
            return total + jnp.where(mine == 2 * h + 1, full_sum[:, 128:], 0.0)

        total = lax.fori_loop(0, LOCAL // 2, body, jnp.zeros((chunk_rows, 128), F32))
        part[k] = total.reshape(NT, chunk_rows // NT, 128)
        for d in range(1, NT):
            peer = lax.rem(t + d, NT)
            copy = remote(
                part.at[k, peer], rs_in.at[k, d - 1], r_ss.at[k, d - 1], r_rs.at[k, d - 1], at_t(d)
            )
            copy.start()
            sent.append(copy)
            r_copies[k, d] = copy

    def reduce(k):
        for d in range(1, NT):
            r_copies[k, d].wait_recv()
        total = part[k, t]
        for d in range(1, NT):
            total = total + rs_in[k, d - 1]
        gath[k, t] = total.astype(BF16)
        for d in range(1, NT):
            copy = remote(
                gath.at[k, t], gath.at[k, t], g_ss.at[k, d - 1], g_rs.at[k, d - 1], at_t(d)
            )
            copy.start()
            sent.append(copy)
            g_copies[k, d] = copy

    def expand(k):
        for d in range(1, NT):
            g_copies[k, d].wait_recv()
        mine = adapter_of((chunk_rows, 128))
        shrunk = gath[k].reshape(chunk_rows, 128).astype(F32)
        spread = jnp.concatenate(
            [jnp.where(mine == e, shrunk, 0.0).astype(BF16) for e in range(LOCAL)], axis=1
        )
        delta = dot(spread, umat[...]).astype(BF16)
        for i in range(2):
            q = 2 * k + i
            mine = delta[i * NY * PAIR : (i + 1) * NY * PAIR]
            dout[q] = mine
            if ORDER[q] in POOLED or ORDER[q] == 0:
                land = rmid if ORDER[q] in POOLED else fin
                land[q, 0:PAIR] = mine[0:PAIR]
                for d in range(1, NY):
                    send(yr_copies, (q, d), remote(
                        dout.at[q, half(d)], land.at[q, half(d)],
                        yr_ss.at[q, d - 1], yr_rs.at[q, d - 1], at_yz(-d, 0),
                    ))
            else:
                send(zr_copies, q, remote(
                    dout.at[q], rmid.at[q], zr_ss.at[q], zr_rs.at[q], at_yz(0, -ORDER[q])
                ))

    def unpack(k):
        for q in (2 * k, 2 * k + 1):
            if ORDER[q] not in POOLED:
                continue
            for d in range(1, NY):
                yr_copies[q, d].wait_recv()
            have = jnp.transpose(meta_in[q])[0:SLOTS, 0:1]
            want = lax.broadcasted_iota(jnp.int32, (SLOTS, NY * PAIR), 1).astype(F32) + 1.0
            pick = jnp.where(want == have, 1.0, 0.0).astype(BF16)
            zret[q, 0:SLOTS] = dot(pick, rmid[q]).astype(BF16)
            send(zr_copies, q, remote(
                zret.at[q, span], fin.at[q, span], zr_ss.at[q], zr_rs.at[q], at_yz(0, -ORDER[q])
            ))

    def back(k):
        for q in (2 * k, 2 * k + 1):
            zr_copies[q].wait_recv()
            for d in range(1, NY):
                send(yr_copies, (q, d), remote(
                    rmid.at[q, half(d)], fin.at[q, half(d)],
                    yr_ss.at[q, d - 1], yr_rs.at[q, d - 1], at_yz(-d, 0),
                ))
            fin[q, 0:PAIR] = rmid[q, 0:PAIR]

    tile = 256

    def collect(k, last):
        for q in (2 * k, 2 * k + 1):
            if ORDER[q] in POOLED:
                zr_copies[q].wait_recv()
                continue
            for d in range(1, NY):
                yr_copies[q, d].wait_recv()

        count = SIZE[2 * k] + SIZE[2 * k + 1]
        rows_in = jnp.concatenate([fin[q, 0 : SIZE[q]] for q in (2 * k, 2 * k + 1)], axis=0)

        def body(r, carry):
            span = pl.ds(pl.multiple_of(r * tile, tile), tile)
            total = acc[span, :] + dot(picks[k, span, 0:count], rows_in)
            if last:
                out[span, :] = total.astype(BF16)
            else:
                acc[span, :] = total
            return carry

        lax.fori_loop(0, rows // tile, body, 0)

    def choose(k):
        count = SIZE[2 * k] + SIZE[2 * k + 1]

        def body(r, carry):
            span = pl.ds(pl.multiple_of(r * tile, tile), tile)
            slot_id = (lax.broadcasted_iota(jnp.int32, (tile, count), 1) + START[2 * k]).astype(F32)
            picks[k, span, 0:count] = jnp.where(slot_id == tgt_col[span, 0:1], 1.0, 0.0).astype(BF16)
            return carry

        lax.fori_loop(0, rows // tile, body, 0)

    def base(first, stop):
        def step(s, carry):
            slot = lax.rem(s, 2)
            for copy in base_copies(s, slot):
                copy.wait()

            @pl.when(s + 1 < steps)
            def _():
                for copy in base_copies(s + 1, 1 - slot):
                    copy.start()

            w32[...] = wbuf[slot].astype(F32)
            rhs = jnp.concatenate(
                [w32[pl.ds(j, width, stride=2), :].astype(BF16) for j in range(2)], axis=1
            )

            def body(r, c):
                span = pl.ds(pl.multiple_of(r * tile, tile), tile)
                acc[span, :] += dot(tok[slot, span, :], rhs)
                return c

            lax.fori_loop(0, rows // tile, body, 0)
            return carry

        lax.fori_loop(first, stop, step, 0)

    assign()
    pack(0)
    pack(2, 3)
    dropped = jnp.where(tgt_row[...] < 0, 1.0, 0.0)
    flags[0] = jnp.broadcast_to(jnp.max(dropped, axis=1, keepdims=True), flags.shape[1:])
    for d in range(1, NZ):
        send(f_copies, d, remote(
            flags.at[0], flags.at[d], f_ss.at[d - 1], f_rs.at[d - 1], at_yz(0, d)
        ))
    a_copy.start()
    for copy in base_copies(0, 0):
        copy.start()
    pack(4, 5)
    pack(6, 7)
    pack(1)
    rank_row = lax.broadcasted_iota(jnp.int32, up.shape, 0) % 128
    umat[:, 0:128] = jnp.where(rank_row < 64, up[...].astype(F32), 0.0).astype(BF16)
    umat[:, 128:256] = jnp.where(rank_row < 64, 0.0, up[...].astype(F32)).astype(BF16)
    acc[...] = jnp.zeros_like(acc)
    tgt_col[...] = jnp.transpose(jnp.broadcast_to(tgt_row[...].astype(F32), (8, rows)))
    base(0, 5)
    for d in range(1, NZ):
        f_copies[d].wait_recv()
    flags[NZ] = jnp.max(flags[0:NZ], axis=0)
    for d in range(1, NY):
        send(f_copies, NZ + d, remote(
            flags.at[NZ], flags.at[NZ + d], f_ss.at[NZ + d - 2], f_rs.at[NZ + d - 2], at_yz(d, 0)
        ))
    choose(0)
    choose(1)
    a_copy.wait()
    repack(0)
    forward(2)
    project(0)
    forward(3)
    reduce(0)
    base(5, 7)
    expand(0)
    base(7, 8)
    unpack(0)
    repack(1)
    choose(2)
    choose(3)
    project(1)
    reduce(1)
    project(2)
    expand(1)
    reduce(2)
    project(3)
    unpack(1)
    expand(2)
    collect(0, False)
    reduce(3)
    expand(3)
    back(2)
    collect(1, False)
    back(3)
    collect(2, False)
    collect(3, True)
    for d in range(1, NY):
        f_copies[NZ + d].wait_recv()
    over[0, 0] = jnp.max(flags[NZ : NZ + NY])
    for copy in sent:
        copy.wait_send()


def general(
    tokens, request_adapter, storage_position, key_value_weight, adapter_down_maps, adapter_up_maps
):
    rows, full = tokens.shape
    groups = NY * NZ
    width, rank = adapter_down_maps.shape[1:]
    kv = key_value_weight.shape[2]
    table = jnp.arange(storage_position.shape[0], dtype=jnp.int32)
    position = jnp.sum(
        jnp.where(request_adapter == table[None, :], storage_position[None, :], 0), axis=1
    )
    seq = jnp.arange(rows, dtype=jnp.int32)
    earlier = (position[:, None] == position[None, :]) & (seq[None, :] < seq[:, None])
    place = jnp.sum(earlier.astype(jnp.int32), axis=1)
    target = position // LOCAL * PAIR + position % LOCAL * MOST + place
    own = lax.dynamic_slice_in_dim(tokens, lax.axis_index("tp") * width, width, 1)
    outgoing = jnp.zeros((groups * PAIR, width), BF16).at[target].set(own)
    arrived = lax.all_to_all(
        outgoing.reshape(groups, PAIR, width), "req", split_axis=0, concat_axis=0, tiled=True
    )
    partial = jnp.einsum(
        "uebf,efn->uebn", arrived.reshape(groups, LOCAL, MOST, width), adapter_down_maps,
        preferred_element_type=F32,
    )
    shrunk = lax.psum(partial, "tp").astype(BF16)
    delta = jnp.einsum(
        "fipst,istk->fipsk", shrunk.reshape(groups, LOCAL, MOST, 2, rank // 2), adapter_up_maps,
        preferred_element_type=F32,
    ).astype(BF16)
    returned = lax.all_to_all(
        delta.reshape(groups, PAIR, 2, kv), "req", split_axis=0, concat_axis=0, tiled=True
    )
    own_delta = returned.reshape(groups * PAIR, 2, kv)[target]
    base = dot(tokens, key_value_weight.reshape(full, 2 * kv)).reshape(rows, 2, kv)
    return (base + own_delta.astype(F32)).astype(BF16)


def local(
    tokens, request_adapter, storage_position, key_value_weight, adapter_down_maps, adapter_up_maps
):
    rows, full = tokens.shape
    width = adapter_down_maps.shape[1]
    kv = key_value_weight.shape[2]
    adapters = storage_position.shape[0]
    chunk = 2 * NY * PAIR
    vmem = pl.BlockSpec(memory_space=pltpu.VMEM)
    hbm = pl.BlockSpec(memory_space=pl.ANY)
    dma = pltpu.SemaphoreType.DMA
    result, over = pl.pallas_call(
        kernel,
        out_shape=(
            jax.ShapeDtypeStruct((rows, 2 * kv), BF16),
            jax.ShapeDtypeStruct((1, 1), F32),
        ),
        in_specs=[vmem, vmem, vmem, hbm, hbm, hbm],
        out_specs=(vmem, pl.BlockSpec(memory_space=pltpu.SMEM)),
        scratch_shapes=[
            pltpu.VMEM((rows, width), BF16),
            pltpu.VMEM((2, rows, width), BF16),
            pltpu.VMEM((2, 2 * width, kv), BF16),
            pltpu.VMEM((2 * width, kv), F32),
            pltpu.VMEM(adapter_down_maps.shape, BF16),
            pltpu.VMEM((LOCAL * 128, 2 * kv), BF16),
            pltpu.VMEM((rows, 2 * kv), F32),
            pltpu.VMEM((1, rows), jnp.int32),
            pltpu.VMEM((1, rows), F32),
            pltpu.VMEM((rows, 8), F32),
            pltpu.VMEM((CHUNKS, rows, 2 * NY * PAIR), BF16),
            pltpu.VMEM((NZ, NY * PAIR, width), BF16),
            pltpu.VMEM((NZ, 8, 256), F32),
            pltpu.VMEM((NZ, NY * PAIR, width), BF16),
            pltpu.VMEM((NZ, 8, 256), F32),
            pltpu.VMEM((NZ, NY * PAIR, width), BF16),
            pltpu.VMEM((NZ, NY * PAIR, width), BF16),
            pltpu.VMEM((CHUNKS, NT, chunk // NT, 128), F32),
            pltpu.VMEM((CHUNKS, NT - 1, chunk // NT, 128), F32),
            pltpu.VMEM((CHUNKS, NT, chunk // NT, 128), BF16),
            pltpu.VMEM((NZ, NY * PAIR, 2 * kv), BF16),
            pltpu.VMEM((NZ, NY * PAIR, 2 * kv), BF16),
            pltpu.VMEM((NZ, NY * PAIR, 2 * kv), BF16),
            pltpu.VMEM((NZ, NY * PAIR, 2 * kv), BF16),
            pltpu.VMEM((NZ + NY, 8, 128), F32),
            dma, dma, dma((2,)), dma((2,)),
            dma((NZ,)), dma((NZ,)), dma((NZ,)), dma((NZ,)),
            dma((NZ, NY - 1)), dma((NZ, NY - 1)),
            dma((CHUNKS, NT - 1)), dma((CHUNKS, NT - 1)),
            dma((CHUNKS, NT - 1)), dma((CHUNKS, NT - 1)),
            dma((NZ, NY - 1)), dma((NZ, NY - 1)),
            dma((NZ,)), dma((NZ,)),
            dma((NZ + NY - 2,)), dma((NZ + NY - 2,)),
        ],
        compiler_params=pltpu.CompilerParams(
            collective_id=0, has_side_effects=True, vmem_limit_bytes=56 * 2**20
        ),
        cost_estimate=pl.CostEstimate(
            flops=12_000_000_000, bytes_accessed=24_000_000, transcendentals=0
        ),
    )(
        request_adapter.reshape(1, rows), storage_position.reshape(1, adapters),
        adapter_up_maps.reshape(LOCAL * 128, kv),
        tokens, key_value_weight.reshape(2 * full, kv), adapter_down_maps,
    )
    args = (
        tokens, request_adapter, storage_position, key_value_weight, adapter_down_maps,
        adapter_up_maps,
    )
    return lax.cond(
        over[0, 0] > 0, lambda: general(*args), lambda: result.reshape(rows, 2, kv)
    )


def solution(mesh):
    in_specs = (
        P("req", None),
        P("req", None),
        P(),
        P(None, None, "tp"),
        P("req", "tp", None),
        P("req", None, None, "tp"),
    )
    out_specs = P("req", None, "tp")
    return jax.shard_map(local, mesh=mesh, in_specs=in_specs, out_specs=out_specs, check_vma=False)
```
